512 devices in a mesh: req: 32 (over y, z_hi, x), patch: 16 (over z_lo, core).
Axes of the slice: x: 4, y: 4, z: 16 (z_hi: 2, z_lo: 8; z = z_hi * 8 + z_lo), core: 2. Of those that a mesh axis runs over, the one named last changes fastest.
Arguments:
- image_queries: bfloat16 [32, 512, 1152], P('req', 'patch'), may hold values from -256 to 256
- cross_queries: bfloat16 [32, 512, 1152], P('req', 'patch'), may hold values from -256 to 256
- fresh_kv: bfloat16 [32, 512, 2304], P('req', 'patch'), may hold values from -6 to 6
- stale_kv: bfloat16 [32, 512, 2304], P('req', 'patch'), may hold values from -6 to 6
- prompt_states: bfloat16 [32, 300, 4096], P('req', None, 'patch'), may hold values from -6 to 6
- caption_weight: bfloat16 [4096, 1152], P('patch'), may hold values from -0.09375 to 0.09375
- cross_kv_weight: bfloat16 [1152, 2304], P(None, 'patch'), may hold values from -0.1875 to 0.1875
- prompt_lengths: int32 [32], replicated, may hold values from 20 to 300, as said below
- prompt_route: int32 [32], replicated, may hold values from 0 to 31, as said below
Outputs:
- self_out: float32 [32, 512, 1152], P('req', 'patch')
- cross_out: float32 [32, 512, 1152], P('req', 'patch')
The draws below stay inside these ranges and needn't reach their ends.
Inputs may be any that keep to these rules, and one draw needn't show every extreme that they name: `prompt_lengths`: every prompt has at least 20 and at most 300 live tokens; some prompt has exactly 300. `prompt_route`: each prompt is used by exactly one request.
All inputs are finite; a program needn't handle non-finite values.
Results may differ from the reference program's by a relative error of at most 0.012.
The reference program's roundings to bfloat16 on the way (of `caption` and `head_states`) count: a program that leaves them out, or rounds other values in their place, can miss the bound.
Values may be sent and summed in bfloat16 or wider, within the bound.
A program may use at most 64 MiB of HBM per device.

```python
import math
import jax
import jax.numpy as jnp
from jax import lax

D = 1152
HEADS = 16
TD = 4096
PMAX = 300
LMIN = 20
TOK_DEV = 32
HD = 72
SEQ = 512
N_REQS = 32
N_PATCH = 16


def query_field(key, largest):
    noise_key, scale_key = jax.random.split(key)
    normal_part = jnp.clip(jax.random.normal(noise_key, (N_REQS, SEQ, HEADS, HD), jnp.float32), -4.0, 4.0)
    row_scale = jnp.exp(jax.random.uniform(scale_key, (N_REQS, SEQ, HEADS, 1), jnp.float32, 0.0, math.log(largest)))
    return (normal_part * row_scale).reshape(N_REQS, SEQ, D).astype(jnp.bfloat16)


def draw_image_queries(key, part):
    key = jax.random.fold_in(key, 11)
    return query_field(key, 1.5)


def draw_cross_queries(key, part):
    key = jax.random.fold_in(key, 23)
    return query_field(key, 1.5)


def draw_prompt_lengths(key, part):
    key = jax.random.fold_in(key, 37)
    length_key, picked_key = jax.random.split(key)
    drawn = jax.random.randint(length_key, (N_REQS,), LMIN, PMAX + 1, dtype=jnp.int32)
    picked = jax.random.permutation(picked_key, N_REQS)
    drawn = drawn.at[picked[0]].set(PMAX)
    return drawn.at[picked[1]].set(LMIN)


def draw_prompt_route(key, part):
    key = jax.random.fold_in(key, 53)
    start_key, order_key = jax.random.split(key)
    first = jax.random.randint(start_key, (), 0, N_REQS, dtype=jnp.int32)
    index = jnp.arange(N_REQS, dtype=jnp.int32)
    fixed_pos = jnp.stack([first, (first + 1) % N_REQS, (first + 2) % N_REQS]).astype(jnp.int32)
    fixed_val = jnp.stack([(first + N_REQS // 2) % N_REQS, first, (first + 3) % N_REQS]).astype(jnp.int32)
    pos_taken = jnp.any(index[:, None] == fixed_pos[None, :], axis=1)
    val_taken = jnp.any(index[:, None] == fixed_val[None, :], axis=1)
    free_pos = jnp.argsort(jnp.where(pos_taken, N_REQS + index, index)).astype(jnp.int32)
    shuffled = jax.random.permutation(order_key, N_REQS).astype(jnp.int32)
    order = jnp.argsort(val_taken[shuffled].astype(jnp.int32), stable=True)
    free_val = shuffled[order]
    route = jnp.zeros((N_REQS,), jnp.int32)
    route = route.at[free_pos[:N_REQS - 3]].set(free_val[:N_REQS - 3])
    return route.at[fixed_pos].set(fixed_val)


def shard_levels(own_key, shape, shards, smallest, high):
    loudness = 1.0
    for axis_at, blocks in shards:
        heights = jax.random.uniform(jax.random.fold_in(jax.random.fold_in(own_key, 6), axis_at), (blocks,), jnp.float32, smallest / len(shards), high / len(shards))
        loudness = loudness * jnp.repeat(jnp.exp(heights), shape[axis_at] // blocks).reshape((-1,) + (1,) * (len(shape) - 1 - axis_at))
    return loudness


def bell_draw(stream_key, shape, spread, limit, cuts=(), kind=jnp.bfloat16):
    gain = shard_levels(stream_key, shape, cuts, -0.22, 0.18) if cuts else 1.0
    values = jax.random.normal(stream_key, shape, jnp.float32) * spread * gain
    return jnp.minimum(jnp.maximum(values, -limit), limit).astype(kind)


def setup_inputs(seed: int = 0) -> dict:
    seeds = jax.random.split(jax.random.key(seed), 10)
    image_queries = draw_image_queries(jax.random.fold_in(seeds[9], 71), 0)
    cross_queries = draw_cross_queries(jax.random.fold_in(seeds[9], 71), 0)
    fresh_kv = bell_draw(seeds[2], (N_REQS, SEQ, 2 * D), 1.0, 6.0, ((0, 32), (1, 16)))
    stale_kv = bell_draw(seeds[3], (N_REQS, SEQ, 2 * D), 1.0, 6.0, ((0, 32), (1, 16)))
    prompt_states = bell_draw(seeds[4], (N_REQS, PMAX, TD), 1.0, 6.0, ((0, 32), (2, 16)))
    caption_weight = bell_draw(seeds[5], (TD, D), TD ** -0.5, 0.09375, ((0, 16),))
    cross_kv_weight = bell_draw(seeds[6], (D, 2 * D), D ** -0.5, 0.1875, ((1, 16),))
    prompt_lengths = draw_prompt_lengths(jax.random.fold_in(seeds[9], 71), 0)
    prompt_route = draw_prompt_route(jax.random.fold_in(seeds[9], 71), 0)
    return {"image_queries": image_queries, "cross_queries": cross_queries, "fresh_kv": fresh_kv, "stale_kv": stale_kv, "prompt_states": prompt_states, "caption_weight": caption_weight, "cross_kv_weight": cross_kv_weight, "prompt_lengths": prompt_lengths, "prompt_route": prompt_route}


masked_score = -1e30


def attend(queries, key_rows, values, visible):
    scores = jnp.einsum('qhd,khd->qhk', queries.astype(jnp.float32), key_rows.astype(jnp.float32)) * (HD ** -0.5)
    scores = jnp.where(visible[None, None, :], scores, masked_score)
    highest = jnp.max(scores, axis=-1, keepdims=True)
    weights = jnp.exp(scores - highest)
    weight_sum = jnp.sum(weights, axis=-1)
    rounded = lax.optimization_barrier(weights.astype(jnp.bfloat16))
    blended = jnp.einsum('qhk,khd->qhd', rounded.astype(jnp.float32), values.astype(jnp.float32))
    return blended / weight_sum[..., None]


def reference(image_queries, cross_queries, fresh_kv, stale_kv, prompt_states, caption_weight, cross_kv_weight, prompt_lengths, prompt_route):
    def one_request(request_items):
        queries, cross_rows, fresh_rows, stale_rows, source = request_items
        prompt = lax.dynamic_index_in_dim(prompt_states, source, 0, keepdims=False)
        length = lax.dynamic_index_in_dim(prompt_lengths, source, 0, keepdims=False)
        caption = jax.nn.gelu(jnp.dot(prompt, caption_weight, preferred_element_type=jnp.float32), approximate=True).astype(jnp.bfloat16)
        head_states = jnp.dot(caption, cross_kv_weight, preferred_element_type=jnp.float32).astype(jnp.bfloat16)
        head_states = head_states.reshape(PMAX, HEADS, 2, HD)
        prompt_visible = jnp.arange(PMAX, dtype=jnp.int32) < length
        cross_part = attend(cross_rows.reshape(SEQ, HEADS, HD), head_states[:, :, 0], head_states[:, :, 1], prompt_visible)
        stale_all = stale_rows.reshape(SEQ, 2, HEADS, HD)
        fresh_all = fresh_rows.reshape(SEQ, 2, HEADS, HD)
        query_all = queries.reshape(SEQ, HEADS, HD)
        everyone = jnp.ones((SEQ,), dtype=bool)

        def one_patch(patch_index):
            begin_row = (patch_index * TOK_DEV).astype(jnp.int32)
            own_keys = lax.dynamic_slice_in_dim(fresh_all, begin_row, TOK_DEV, 0)
            merged = lax.dynamic_update_slice_in_dim(stale_all, own_keys, begin_row, 0)
            query_block = lax.dynamic_slice_in_dim(query_all, begin_row, TOK_DEV, 0)
            return attend(query_block, merged[:, 0], merged[:, 1], everyone)

        self_part = lax.map(one_patch, jnp.arange(N_PATCH, dtype=jnp.int32))
        return self_part.reshape(SEQ, D), cross_part.reshape(SEQ, D)

    self_out, cross_out = lax.map(one_request, (image_queries, cross_queries, fresh_kv, stale_kv, prompt_route))
    return self_out, cross_out
```

```python
import functools

import jax
import jax.numpy as jnp
from jax import lax
from jax.experimental import pallas as pl
from jax.experimental.pallas import tpu as pltpu
from jax.sharding import PartitionSpec as P

HEADS = 16
HD = 72
LANES = 128
TILE = 16
TILES = 11
LINE = 8
CUTS = ((0, 6), (6, 5))
masked_score = -1e30
MESH = pl.DeviceIdType.MESH


def kernel(
    dims,
    route_ref,
    lengths_ref,
    prompt_ref,
    caption_w_ref,
    kv_w_ref,
    image_q_ref,
    cross_q_ref,
    fresh_ref,
    stale_ref,
    self_out_ref,
    cross_out_ref,
    part,
    sib_part,
    from_low,
    from_high,
    routed,
    y_send,
    y_recv,
    caption,
    cq_send,
    cq_recv,
    sf_send,
    sf_recv,
    so_send,
    so_recv,
    co_send,
    co_recv,
    sib_sems,
    low_sems,
    high_sems,
    h_sems,
    x_sems,
    y_sems,
    up_sems,
    down_sems,
    gather_recv,
    twin_sems,
    cq_sems,
    sf_sems,
    so_sems,
    co_sems,
):
    n_y, n_h, n_x = dims
    me_r = lax.axis_index("req")
    me_p = lax.axis_index("patch")
    y = me_r // (n_h * n_x)
    h = (me_r // n_x) % n_h
    x = me_r % n_x
    z = me_p // 2
    c = me_p % 2
    u = z + h * (LINE - 1 - 2 * z)

    def on_line(pos, core):
        return 2 * (pos + h * (LINE - 1 - 2 * pos)) + core

    def patch_peer(i):
        return {"patch": (me_p + i) % (2 * LINE)}

    twin = {"patch": 2 * z + 1 - c}
    upper = {"patch": on_line(jnp.minimum(u + 1, LINE - 1), c)}
    lower = {"patch": on_line(jnp.maximum(u - 1, 0), c)}
    half_peer = {"req": me_r + n_x * (1 - 2 * h), "patch": 2 * (LINE - 1 - z) + c}

    def x_peer(i):
        return {"req": me_r - x + (x + i) % n_x}

    def y_peer(i):
        return {"req": ((y + i) % n_y) * (n_h * n_x) + h * n_x + x}

    def copy(src, dst, send, recv, device):
        return pltpu.make_async_remote_copy(
            src_ref=src, dst_ref=dst, send_sem=send, recv_sem=recv, device_id=device, device_id_type=MESH
        )

    barrier = pltpu.get_barrier_semaphore()
    greeted = 0
    for device in (
        [patch_peer(i) for i in range(1, 2 * LINE)]
        + [half_peer]
        + [x_peer(i) for i in range(1, n_x)]
        + [y_peer(i) for i in range(1, n_y)]
    ):
        pl.semaphore_signal(barrier, inc=1, device_id=device, device_id_type=MESH)
        greeted += 1
    pl.semaphore_wait(barrier, greeted)

    prompt = prompt_ref[0]
    rows = prompt.shape[0]
    row_tiles = -(-rows // TILE)
    prompt = jnp.concatenate(
        [prompt, jnp.zeros((row_tiles * TILE - rows, prompt.shape[1]), prompt.dtype)], axis=0
    )
    width = caption_w_ref.shape[1]
    col_tiles = width // LANES

    def place(i, j):
        piece, at = divmod(i * col_tiles + j, TILES)
        return piece // LINE, piece % LINE, at

    group = 3
    for j0 in range(0, col_tiles, group):
        block = jnp.dot(
            prompt, caption_w_ref[:, j0 * LANES : (j0 + group) * LANES], preferred_element_type=jnp.float32
        )
        for i in range(row_tiles):
            for j in range(group):
                part[place(i, j0 + j)] = block[i * TILE : (i + 1) * TILE, j * LANES : (j + 1) * LANES]
    for t in range(row_tiles * col_tiles, 2 * LINE * TILES):
        part[t // (LINE * TILES), (t // TILES) % LINE, t % TILES] = jnp.zeros((TILE, LANES), jnp.float32)

    to_twin = copy(part.at[1 - c], sib_part, sib_sems.at[0], sib_sems.at[1], twin)
    to_twin.start()

    tok = image_q_ref.shape[1]
    pad_c = jnp.zeros((tok, LANES - HD), jnp.bfloat16)
    pad_s = jnp.zeros((tok, 3 * LANES - 5 * HD), jnp.bfloat16)
    for n in range(HEADS):
        a, b = n * HD, (n + 1) * HD
        cq_send[n] = jnp.concatenate([cross_q_ref[0, :, a:b], pad_c], axis=1)
        sf_send[n] = jnp.concatenate(
            [
                image_q_ref[0, :, a:b],
                stale_ref[0, :, a:b],
                stale_ref[0, :, width + a : width + b],
                fresh_ref[0, :, a:b],
                fresh_ref[0, :, width + a : width + b],
                pad_s,
            ],
            axis=1,
        )

    def exchange(send, recv, sems, i):
        peer = (me_p + i) % (2 * LINE)
        return copy(send.at[peer], recv.at[me_p], sems.at[0, i], sems.at[1, i], {"patch": peer})

    def arrival(send, recv, sems, i):
        origin = (me_p - i + 2 * LINE) % (2 * LINE)
        return copy(send.at[origin], recv.at[origin], sems.at[0, i], sems.at[1, i], {"patch": origin})

    def start_exchange(send, recv, sems):
        recv[me_p] = send[me_p]

        def step(i, _):
            exchange(send, recv, sems, i).start()
            return 0

        lax.fori_loop(1, 2 * LINE, step, 0)

    def end_exchange(send, recv, sems):
        def step(i, _):
            arrival(send, recv, sems, i).wait_recv()
            return 0

        lax.fori_loop(1, 2 * LINE, step, 0)

    def drain_exchange(send, recv, sems):
        def step(i, _):
            exchange(send, recv, sems, i).wait_send()
            return 0

        lax.fori_loop(1, 2 * LINE, step, 0)

    to_twin.wait_recv()
    to_twin.wait_send()
    sums = part.at[c]

    def add_twin(i, _):
        sums[i] = sums[i] + sib_part[i]
        return 0

    lax.fori_loop(0, LINE, add_twin, 0)

    def go_up(d, k):
        a, m = CUTS[k]
        cut = pl.ds(a, m)
        return copy(sums.at[d, cut], from_low.at[d, cut], low_sems.at[0, d, k], low_sems.at[1, d, k], upper)

    def go_down(d, k):
        a, m = CUTS[k]
        cut = pl.ds(a, m)
        return copy(sums.at[d, cut], from_high.at[d, cut], high_sems.at[0, d, k], high_sems.at[1, d, k], lower)

    def reduce_step(t, _):
        for k, (a, m) in enumerate(CUTS):
            cut = pl.ds(a, m)

            @pl.when(t >= u)
            def _():
                d = LINE - 1 - t + u

                @pl.when(u > 0)
                def _():
                    go_up(d, k).wait_recv()
                    sums[d, cut] = sums[d, cut] + from_low[d, cut]

                @pl.when(d > u)
                def _():
                    go_up(d, k).start()

            @pl.when(t >= LINE - 1 - u)
            def _():
                d = t - (LINE - 1) + u

                @pl.when(u < LINE - 1)
                def _():
                    go_down(d, k).wait_recv()
                    sums[d, cut] = sums[d, cut] + from_high[d, cut]

                @pl.when(d < u)
                def _():
                    go_down(d, k).start()

        return 0

    lax.fori_loop(0, LINE, reduce_step, 0)

    piece = jax.nn.gelu(sums[u], approximate=True).astype(jnp.bfloat16)
    routed[x, h] = piece
    to_half = copy(routed.at[x, h], routed.at[x, h], h_sems.at[0], h_sems.at[1], half_peer)
    to_half.start()

    def x_copy(i, half):
        return copy(routed.at[x, half], routed.at[x, half], x_sems.at[0, half, i], x_sems.at[1, half, i], x_peer(i))

    def x_arrival(i, half):
        origin = (x - i + n_x) % n_x
        return copy(routed.at[x, half], routed.at[origin, half], x_sems.at[0, half, i], x_sems.at[1, half, i], x_peer(i))

    for i in range(1, n_x):
        x_copy(i, h).start()
    start_exchange(cq_send, cq_recv, cq_sems)
    start_exchange(sf_send, sf_recv, sf_sems)
    half_in = copy(routed.at[x, 1 - h], routed.at[x, 1 - h], h_sems.at[0], h_sems.at[1], half_peer)
    half_in.wait_recv()
    for i in range(1, n_x):
        x_copy(i, 1 - h).start()
    for i in range(1, n_x):
        x_arrival(i, h).wait_recv()
        x_arrival(i, 1 - h).wait_recv()

    def wanted(i):
        target = ((y + i) % n_y) * (n_h * n_x) + h * n_x + x
        source = route_ref[target]
        return routed[lax.rem(source, n_x), lax.rem(lax.div(source, n_x), n_h)]

    def y_copy(i):
        return copy(y_send.at[i], y_recv.at[y], y_sems.at[0, i], y_sems.at[1, i], y_peer(i))

    def y_arrival(i):
        return copy(y_send.at[i], y_recv.at[(y - i + n_y) % n_y], y_sems.at[0, i], y_sems.at[1, i], y_peer(i))

    for i in range(1, n_y):
        y_send[i] = wanted(i)
        y_copy(i).start()
    y_recv[y] = wanted(0)
    for i in range(1, n_y):
        y_arrival(i).wait_recv()
    source = route_ref[me_r]
    caption[c, u] = y_recv[lax.div(source, n_h * n_x)]

    def to_upper(q, k):
        a, m = CUTS[k]
        ref = caption.at[c, q, pl.ds(a, m)]
        return copy(ref, ref, up_sems.at[q, k], gather_recv.at[q, k], upper)

    def to_lower(q, k):
        a, m = CUTS[k]
        ref = caption.at[c, q, pl.ds(a, m)]
        return copy(ref, ref, down_sems.at[q, k], gather_recv.at[q, k], lower)

    def to_other_core(core, q, k):
        a, m = CUTS[k]
        ref = caption.at[core, q, pl.ds(a, m)]
        return copy(ref, ref, twin_sems.at[0, q, k], twin_sems.at[1, q, k], twin)

    def gather_step(t, _):
        for k in range(len(CUTS)):

            @pl.when(t <= u)
            def _():
                q = u - t

                @pl.when(t > 0)
                def _():
                    to_upper(q, k).wait_recv()

                @pl.when(u < LINE - 1)
                def _():
                    to_upper(q, k).start()

                to_other_core(c, q, k).start()

            @pl.when(t <= LINE - 1 - u)
            def _():
                q = u + t

                @pl.when(t > 0)
                def _():
                    to_lower(q, k).wait_recv()

                @pl.when(u > 0)
                def _():
                    to_lower(q, k).start()

                @pl.when(t > 0)
                def _():
                    to_other_core(c, q, k).start()

        return 0

    lax.fori_loop(0, LINE, gather_step, 0)

    end_exchange(sf_send, sf_recv, sf_sems)
    seq = 2 * LINE * tok
    whole = sf_recv[...].reshape(seq, 3 * LANES)
    queries, keys, values = whole[:, :HD], whole[:, HD : 2 * HD], whole[:, 2 * HD : 3 * HD]
    new_keys, new_values = whole[:, 3 * HD : 4 * HD], whole[:, 4 * HD : 5 * HD]
    contract_last = (((1,), (1,)), ((), ()))
    chunk = LANES
    own = (
        lax.broadcasted_iota(jnp.int32, (chunk, chunk), 0) // tok
        == lax.broadcasted_iota(jnp.int32, (chunk, chunk), 1) // tok
    )
    zero = jnp.zeros((), jnp.bfloat16)

    def blended(scores, head_values):
        weights = jnp.exp(scores - jnp.max(scores, axis=-1, keepdims=True))
        return weights, jnp.sum(weights, axis=-1, keepdims=True)

    out_pad = jnp.zeros((chunk, LANES - HD), jnp.bfloat16)
    per = chunk // tok
    for i in range(seq // chunk):
        a, b = i * chunk, (i + 1) * chunk
        scores = lax.dot_general(queries[a:b], keys, contract_last, preferred_element_type=jnp.float32)
        mine = lax.dot_general(queries[a:b], new_keys[a:b], contract_last, preferred_element_type=jnp.float32)
        mixed = [jnp.where(own, mine, scores[:, a:b])]
        if a > 0:
            mixed = [scores[:, :a]] + mixed
        if b < seq:
            mixed = mixed + [scores[:, b:]]
        scores = jnp.concatenate(mixed, axis=1) * HD ** (-0.5)
        weights, total = blended(scores, values)
        weights = weights.astype(jnp.bfloat16)
        near = weights[:, a:b]
        mixed = [jnp.where(own, zero, near)]
        if a > 0:
            mixed = [weights[:, :a]] + mixed
        if b < seq:
            mixed = mixed + [weights[:, b:]]
        result = jnp.dot(jnp.concatenate(mixed, axis=1), values, preferred_element_type=jnp.float32)
        result = result + jnp.dot(
            jnp.where(own, near, zero), new_values[a:b], preferred_element_type=jnp.float32
        )
        result = (result / total).astype(jnp.bfloat16)
        so_send[i * per : (i + 1) * per] = jnp.concatenate([result, out_pad], axis=1).reshape(per, tok, LANES)
    start_exchange(so_send, so_recv, so_sems)

    end_exchange(cq_send, cq_recv, cq_sems)

    def twin_wait(q, _):
        for k in range(len(CUTS)):
            to_other_core(1 - c, q, k).wait_recv()
        return 0

    lax.fori_loop(0, LINE, twin_wait, 0)
    caption_rows = jnp.concatenate(
        [jnp.concatenate([caption[place(i, j)] for j in range(col_tiles)], axis=1) for i in range(row_tiles)], axis=0
    )
    head_states = jnp.dot(caption_rows, kv_w_ref[...], preferred_element_type=jnp.float32).astype(jnp.bfloat16)
    prompt_keys, prompt_values = head_states[:, :HD], head_states[:, HD : 2 * HD]
    length = lengths_ref[source]
    visible = lax.broadcasted_iota(jnp.int32, (1, row_tiles * TILE), 1) < length
    cross_rows = cq_recv[...].reshape(seq, LANES)[:, :HD]
    for i in range(seq // chunk):
        a, b = i * chunk, (i + 1) * chunk
        scores = lax.dot_general(cross_rows[a:b], prompt_keys, contract_last, preferred_element_type=jnp.float32)
        scores = jnp.where(visible, scores * HD ** (-0.5), masked_score)
        weights, total = blended(scores, prompt_values)
        result = jnp.dot(weights.astype(jnp.bfloat16), prompt_values, preferred_element_type=jnp.float32)
        result = (result / total).astype(jnp.bfloat16)
        co_send[i * per : (i + 1) * per] = jnp.concatenate([result, out_pad], axis=1).reshape(per, tok, LANES)
    start_exchange(co_send, co_recv, co_sems)

    end_exchange(so_send, so_recv, so_sems)
    self_out_ref[0] = jnp.concatenate([so_recv[n][:, :HD].astype(jnp.float32) for n in range(HEADS)], axis=1)
    end_exchange(co_send, co_recv, co_sems)
    cross_out_ref[0] = jnp.concatenate([co_recv[n][:, :HD].astype(jnp.float32) for n in range(HEADS)], axis=1)

    for k in range(len(CUTS)):

        def drain(q, _):
            @pl.when(q > u)
            def _():
                go_up(q, k).wait_send()

            @pl.when(q < u)
            def _():
                go_down(q, k).wait_send()

            @pl.when((q <= u) & (u < LINE - 1))
            def _():
                to_upper(q, k).wait_send()

            @pl.when((q >= u) & (u > 0))
            def _():
                to_lower(q, k).wait_send()

            to_other_core(c, q, k).wait_send()
            return 0

        lax.fori_loop(0, LINE, drain, 0)
    to_half.wait_send()
    for i in range(1, n_x):
        x_copy(i, h).wait_send()
        x_copy(i, 1 - h).wait_send()
    for i in range(1, n_y):
        y_copy(i).wait_send()
    drain_exchange(cq_send, cq_recv, cq_sems)
    drain_exchange(sf_send, sf_recv, sf_sems)
    drain_exchange(so_send, so_recv, so_sems)
    drain_exchange(co_send, co_recv, co_sems)


def shards(
    dims,
    image_queries,
    cross_queries,
    fresh_kv,
    stale_kv,
    prompt_states,
    caption_weight,
    cross_kv_weight,
    prompt_lengths,
    prompt_route,
):
    n_y, n_h, n_x = dims
    tok, width = image_queries.shape[1:]
    piece = (TILES, TILE, LANES)
    dma = pltpu.SemaphoreType.DMA
    vmem = pl.BlockSpec(memory_space=pltpu.VMEM)
    smem = pl.BlockSpec(memory_space=pltpu.SMEM)
    f32, bf16 = jnp.float32, jnp.bfloat16
    lines = (LINE, len(CUTS))
    by_head = pltpu.VMEM((HEADS, tok, LANES), bf16)
    by_head_wide = pltpu.VMEM((HEADS, tok, 3 * LANES), bf16)
    return pl.pallas_call(
        functools.partial(kernel, dims),
        out_shape=[jax.ShapeDtypeStruct((1, tok, width), f32)] * 2,
        in_specs=[smem, smem] + [vmem] * 7,
        out_specs=[vmem, vmem],
        scratch_shapes=[
            pltpu.VMEM((2, LINE, *piece), f32),
            pltpu.VMEM((LINE, *piece), f32),
            pltpu.VMEM((LINE, *piece), f32),
            pltpu.VMEM((LINE, *piece), f32),
            pltpu.VMEM((n_x, n_h, *piece), bf16),
            pltpu.VMEM((n_y, *piece), bf16),
            pltpu.VMEM((n_y, *piece), bf16),
            pltpu.VMEM((2, LINE, *piece), bf16),
            by_head,
            by_head,
            by_head_wide,
            by_head_wide,
            by_head,
            by_head,
            by_head,
            by_head,
            dma((2,)),
            dma((2, *lines)),
            dma((2, *lines)),
            dma((2,)),
            dma((2, n_h, n_x)),
            dma((2, n_y)),
            dma(lines),
            dma(lines),
            dma(lines),
            dma((2, *lines)),
            dma((2, HEADS)),
            dma((2, HEADS)),
            dma((2, HEADS)),
            dma((2, HEADS)),
        ],
        compiler_params=pltpu.CompilerParams(
            collective_id=0, has_side_effects=True, vmem_limit_bytes=48 * 1024 * 1024
        ),
    )(
        prompt_route,
        prompt_lengths,
        prompt_states,
        caption_weight,
        cross_kv_weight,
        image_queries,
        cross_queries,
        fresh_kv,
        stale_kv,
    )


def solution(mesh, dims=(4, 2, 4)):
    in_specs = (
        P("req", "patch", None),
        P("req", "patch", None),
        P("req", "patch", None),
        P("req", "patch", None),
        P("req", None, "patch"),
        P("patch", None),
        P(None, "patch"),
        P(),
        P(),
    )
    out_specs = (P("req", "patch", None), P("req", "patch", None))
    return jax.shard_map(
        functools.partial(shards, dims), mesh=mesh, in_specs=in_specs, out_specs=out_specs, check_vma=False
    )
```

```python
import functools

import jax
import jax.numpy as jnp
from jax import lax
from jax.experimental import pallas as pl
from jax.experimental.pallas import tpu as pltpu
from jax.sharding import PartitionSpec as P

HEADS = 16
HD = 72
LANES = 128
TILE = 16
TILES = 11
LINE = 8
HALF = LINE // 2
SUM_CUTS = ((0, 3), (3, 3), (6, 3), (9, 2))
CUTS = ((0, 6), (6, 5))
masked_score = -1e30
MESH = pl.DeviceIdType.MESH


def kernel(
    dims,
    route_ref,
    lengths_ref,
    prompt_hbm,
    caption_w_hbm,
    kv_w_hbm,
    image_q_hbm,
    cross_q_hbm,
    fresh_hbm,
    stale_hbm,
    self_out_ref,
    cross_out_ref,
    prompt_ref,
    caption_w_ref,
    kv_w_ref,
    image_q_ref,
    cross_q_ref,
    fresh_ref,
    stale_ref,
    part,
    sib_part,
    from_low,
    from_high,
    routed,
    y_send,
    y_recv,
    caption,
    cq_send,
    cq_recv,
    sf_send,
    sf_recv,
    so_send,
    so_recv,
    co_send,
    co_recv,
    load_sems,
    sib_sems,
    low_sems,
    high_sems,
    h_sems,
    x_sems,
    y_sems,
    gather_send,
    gather_recv,
    twin_sems,
    cq_sems,
    sf_sems,
    so_sems,
    co_sems,
):
    n_y, n_h, n_x = dims
    me_r = lax.axis_index("req")
    me_p = lax.axis_index("patch")
    y = me_r // (n_h * n_x)
    h = (me_r // n_x) % n_h
    x = me_r % n_x
    z = me_p // 2
    c = me_p % 2
    u = z
    shift = h * HALF

    def piece_of(pos):
        return (pos + shift) % LINE

    def patch_peer(i):
        return {"patch": (me_p + i) % (2 * LINE)}

    twin = {"patch": 2 * z + 1 - c}
    upper = {"patch": 2 * jnp.minimum(u + 1, LINE - 1) + c}
    lower = {"patch": 2 * jnp.maximum(u - 1, 0) + c}
    half_peer = {"req": me_r + n_x * (1 - 2 * h), "patch": 2 * ((z + HALF) % LINE) + c}

    def x_peer(i):
        return {"req": me_r - x + (x + i) % n_x}

    def y_peer(i):
        return {"req": ((y + i) % n_y) * (n_h * n_x) + h * n_x + x}

    def copy(src, dst, send, recv, device):
        return pltpu.make_async_remote_copy(
            src_ref=src, dst_ref=dst, send_sem=send, recv_sem=recv, device_id=device, device_id_type=MESH
        )

    loads = [
        pltpu.make_async_copy(src, dst, load_sems.at[i])
        for i, (src, dst) in enumerate(
            (
                (prompt_hbm, prompt_ref),
                (caption_w_hbm, caption_w_ref),
                (cross_q_hbm, cross_q_ref),
                (image_q_hbm, image_q_ref),
                (stale_hbm, stale_ref),
                (fresh_hbm, fresh_ref),
                (kv_w_hbm, kv_w_ref),
            )
        )
    ]
    barrier = pltpu.get_barrier_semaphore()
    greeted = 0
    for device in (
        [patch_peer(i) for i in range(1, 2 * LINE)]
        + [half_peer]
        + [x_peer(i) for i in range(1, n_x)]
        + [y_peer(i) for i in range(1, n_y)]
    ):
        pl.semaphore_signal(barrier, inc=1, device_id=device, device_id_type=MESH)
        greeted += 1
    for load in loads:
        load.start()

    loads[0].wait()
    loads[1].wait()
    prompt = prompt_ref[0]
    rows = prompt.shape[0]
    row_tiles = -(-rows // TILE)
    prompt = jnp.concatenate(
        [prompt, jnp.zeros((row_tiles * TILE - rows, prompt.shape[1]), prompt.dtype)], axis=0
    )
    width = caption_w_ref.shape[1]
    col_tiles = width // LANES

    def place(i, j):
        piece, at = divmod(i * col_tiles + j, TILES)
        return piece // LINE, piece % LINE, at

    slots = [piece_of(g) for g in range(LINE)]

    group = 3
    for j0 in range(0, col_tiles, group):
        block = jnp.dot(
            prompt, caption_w_ref[:, j0 * LANES : (j0 + group) * LANES], preferred_element_type=jnp.float32
        )
        for i in range(row_tiles):
            for j in range(group):
                core, g, at = place(i, j0 + j)
                part[core, slots[g], at] = block[i * TILE : (i + 1) * TILE, j * LANES : (j + 1) * LANES]
    for t in range(row_tiles * col_tiles, 2 * LINE * TILES):
        part[t // (LINE * TILES), slots[(t // TILES) % LINE], t % TILES] = jnp.zeros((TILE, LANES), jnp.float32)

    to_twin = copy(part.at[1 - c], sib_part, sib_sems.at[0], sib_sems.at[1], twin)
    pl.semaphore_wait(barrier, greeted)
    to_twin.start()
    for load in loads[2:]:
        load.wait()

    tok = image_q_ref.shape[1]
    pad_c = jnp.zeros((tok, LANES - HD), jnp.bfloat16)
    pad_s = jnp.zeros((tok, 3 * LANES - 5 * HD), jnp.bfloat16)
    for n in range(HEADS):
        a, b = n * HD, (n + 1) * HD
        cq_send[n] = jnp.concatenate([cross_q_ref[0, :, a:b], pad_c], axis=1)
        sf_send[n] = jnp.concatenate(
            [
                image_q_ref[0, :, a:b],
                stale_ref[0, :, a:b],
                stale_ref[0, :, width + a : width + b],
                fresh_ref[0, :, a:b],
                fresh_ref[0, :, width + a : width + b],
                pad_s,
            ],
            axis=1,
        )

    def exchange(send, recv, sems, i):
        peer = (me_p + i) % (2 * LINE)
        return copy(send.at[peer], recv.at[me_p], sems.at[0, i], sems.at[1, i], {"patch": peer})

    def arrival(send, recv, sems, i):
        origin = (me_p - i + 2 * LINE) % (2 * LINE)
        return copy(send.at[origin], recv.at[origin], sems.at[0, i], sems.at[1, i], {"patch": origin})

    def start_exchange(send, recv, sems):
        recv[me_p] = send[me_p]

        def step(i, _):
            exchange(send, recv, sems, i).start()
            return 0

        lax.fori_loop(1, 2 * LINE, step, 0)

    def end_exchange(send, recv, sems):
        def step(i, _):
            arrival(send, recv, sems, i).wait_recv()
            return 0

        lax.fori_loop(1, 2 * LINE, step, 0)

    def drain_exchange(send, recv, sems):
        def step(i, _):
            exchange(send, recv, sems, i).wait_send()
            return 0

        lax.fori_loop(1, 2 * LINE, step, 0)

    start_exchange(cq_send, cq_recv, cq_sems)
    start_exchange(sf_send, sf_recv, sf_sems)
    to_twin.wait_recv()
    to_twin.wait_send()
    sums = part.at[c]

    def add_twin(i, _):
        sums[i] = sums[i] + sib_part[i]
        return 0

    lax.fori_loop(0, LINE, add_twin, 0)

    def go_up(d, k):
        a, m = SUM_CUTS[k]
        cut = pl.ds(a, m)
        return copy(sums.at[d, cut], from_low.at[d, cut], low_sems.at[0, d, k], low_sems.at[1, d, k], upper)

    def go_down(d, k):
        a, m = SUM_CUTS[k]
        cut = pl.ds(a, m)
        return copy(sums.at[d, cut], from_high.at[d, cut], high_sems.at[0, d, k], high_sems.at[1, d, k], lower)

    def reduce_step(t, _):
        for k, (a, m) in enumerate(SUM_CUTS):
            cut = pl.ds(a, m)

            @pl.when(t >= u)
            def _():
                d = LINE - 1 - t + u

                @pl.when(u > 0)
                def _():
                    go_up(d, k).wait_recv()
                    sums[d, cut] = sums[d, cut] + from_low[d, cut]

                @pl.when(d > u)
                def _():
                    go_up(d, k).start()

            @pl.when(t >= LINE - 1 - u)
            def _():
                d = t - (LINE - 1) + u

                @pl.when(u < LINE - 1)
                def _():
                    go_down(d, k).wait_recv()
                    sums[d, cut] = sums[d, cut] + from_high[d, cut]

                @pl.when(d < u)
                def _():
                    go_down(d, k).start()

        return 0

    lax.fori_loop(0, LINE, reduce_step, 0)

    def to_half(k):
        ref = routed[k].at[x, h]
        return copy(ref, ref, h_sems.at[0, k], h_sems.at[1, k], half_peer)

    def half_arrival(k):
        ref = routed[k].at[x, 1 - h]
        return copy(ref, ref, h_sems.at[0, k], h_sems.at[1, k], half_peer)

    def x_copy(i, half, k):
        ref = routed[k].at[x, half]
        return copy(ref, ref, x_sems.at[0, k, half, i], x_sems.at[1, k, half, i], x_peer(i))

    def x_arrival(i, half, k):
        ref = routed[k].at[(x - i + n_x) % n_x, half]
        return copy(ref, ref, x_sems.at[0, k, half, i], x_sems.at[1, k, half, i], x_peer(i))

    def wanted(i, k):
        source = route_ref[((y + i) % n_y) * (n_h * n_x) + h * n_x + x]
        return routed[k][lax.rem(source, n_x), lax.rem(lax.div(source, n_x), n_h)]

    def y_copy(i, k):
        return copy(y_send[k].at[i], y_recv[k].at[y], y_sems.at[0, k, i], y_sems.at[1, k, i], y_peer(i))

    def y_arrival(i, k):
        ref = y_recv[k].at[(y - i + n_y) % n_y]
        return copy(ref, ref, y_sems.at[0, k, i], y_sems.at[1, k, i], y_peer(i))

    here = piece_of(u)
    there = piece_of((u + HALF) % LINE)

    def beside(i):
        return (u // HALF) * HALF + (u + i) % HALF

    def tiles_of(core, g, k):
        a, m = CUTS[k]
        return caption.at[core, g, pl.ds(a, m)]

    def spread(g, i, n, k):
        pos = beside(i) if i else (u + HALF) % LINE
        ref = tiles_of(c, g, k)
        return copy(ref, ref, gather_send.at[n, k], gather_recv.at[g, k], {"patch": 2 * pos + c})

    def gathered(g, k):
        ref = tiles_of(c, g, k)
        return copy(ref, ref, gather_send.at[0, k], gather_recv.at[g, k], twin)

    def to_other_core(core, g, k):
        ref = tiles_of(core, g, k)
        return copy(ref, ref, twin_sems.at[0, g, k], twin_sems.at[1, g, k], twin)

    cuts = range(len(CUTS))
    for k, (a, m) in enumerate(CUTS):
        piece = jax.nn.gelu(sums[u, a : a + m], approximate=True).astype(jnp.bfloat16)
        routed[k][x, h] = piece
        to_half(k).start()
        for i in range(1, n_x):
            x_copy(i, h, k).start()
    for k in cuts:
        half_arrival(k).wait_recv()
        for i in range(1, n_x):
            x_copy(i, 1 - h, k).start()
    for k in cuts:
        for i in range(1, n_x):
            x_arrival(i, h, k).wait_recv()
            x_arrival(i, 1 - h, k).wait_recv()
        for i in range(1, n_y):
            y_send[k][i] = wanted(i, k)
            y_copy(i, k).start()
        y_recv[k][y] = wanted(0, k)
    source = route_ref[me_r]
    for k, (a, m) in enumerate(CUTS):
        for i in range(1, n_y):
            y_arrival(i, k).wait_recv()
        caption[c, here, a : a + m] = y_recv[k][lax.div(source, n_h * n_x)]
        for i in range(HALF):
            spread(here, i, i, k).start()
        to_other_core(c, here, k).start()

    end_exchange(sf_send, sf_recv, sf_sems)
    seq = 2 * LINE * tok
    whole = sf_recv[...].reshape(seq, 3 * LANES)
    queries, keys, values = whole[:, :HD], whole[:, HD : 2 * HD], whole[:, 2 * HD : 3 * HD]
    new_keys, new_values = whole[:, 3 * HD : 4 * HD], whole[:, 4 * HD : 5 * HD]
    contract_last = (((1,), (1,)), ((), ()))
    chunk = LANES
    own = (
        lax.broadcasted_iota(jnp.int32, (chunk, chunk), 0) // tok
        == lax.broadcasted_iota(jnp.int32, (chunk, chunk), 1) // tok
    )
    zero = jnp.zeros((), jnp.bfloat16)

    def blended(scores, head_values):
        weights = jnp.exp(scores - jnp.max(scores, axis=-1, keepdims=True))
        return weights, jnp.sum(weights, axis=-1, keepdims=True)

    out_pad = jnp.zeros((chunk, LANES - HD), jnp.bfloat16)
    per = chunk // tok
    for i in range(seq // chunk):
        a, b = i * chunk, (i + 1) * chunk
        scores = lax.dot_general(queries[a:b], keys, contract_last, preferred_element_type=jnp.float32)
        mine = lax.dot_general(queries[a:b], new_keys[a:b], contract_last, preferred_element_type=jnp.float32)
        mixed = [jnp.where(own, mine, scores[:, a:b])]
        if a > 0:
            mixed = [scores[:, :a]] + mixed
        if b < seq:
            mixed = mixed + [scores[:, b:]]
        scores = jnp.concatenate(mixed, axis=1) * HD ** (-0.5)
        weights, total = blended(scores, values)
        weights = weights.astype(jnp.bfloat16)
        near = weights[:, a:b]
        mixed = [jnp.where(own, zero, near)]
        if a > 0:
            mixed = [weights[:, :a]] + mixed
        if b < seq:
            mixed = mixed + [weights[:, b:]]
        result = jnp.dot(jnp.concatenate(mixed, axis=1), values, preferred_element_type=jnp.float32)
        result = result + jnp.dot(
            jnp.where(own, near, zero), new_values[a:b], preferred_element_type=jnp.float32
        )
        result = (result / total).astype(jnp.bfloat16)
        so_send[i * per : (i + 1) * per] = jnp.concatenate([result, out_pad], axis=1).reshape(per, tok, LANES)
    start_exchange(so_send, so_recv, so_sems)

    for k in cuts:
        gathered(there, k).wait_recv()
        for i in range(1, HALF):
            spread(there, i, HALF - 1 + i, k).start()
        to_other_core(c, there, k).start()
    for far in (0, HALF):
        for k in cuts:
            for i in range(1, HALF):
                g = piece_of((beside(i) + far) % LINE)
                gathered(g, k).wait_recv()
                to_other_core(c, g, k).start()

    end_exchange(cq_send, cq_recv, cq_sems)

    def twin_wait(q, _):
        for k in range(len(CUTS)):
            to_other_core(1 - c, q, k).wait_recv()
        return 0

    lax.fori_loop(0, LINE, twin_wait, 0)
    caption_rows = jnp.concatenate(
        [jnp.concatenate([caption[place(i, j)] for j in range(col_tiles)], axis=1) for i in range(row_tiles)], axis=0
    )
    head_states = lax.dot_general(
        caption_rows, kv_w_ref[...], contract_last, preferred_element_type=jnp.float32
    ).astype(jnp.bfloat16)
    prompt_keys, prompt_values = head_states[:, :HD], head_states[:, HD : 2 * HD]
    length = lengths_ref[source]
    visible = lax.broadcasted_iota(jnp.int32, (1, row_tiles * TILE), 1) < length
    cross_rows = cq_recv[...].reshape(seq, LANES)[:, :HD]
    for i in range(seq // chunk):
        a, b = i * chunk, (i + 1) * chunk
        scores = lax.dot_general(cross_rows[a:b], prompt_keys, contract_last, preferred_element_type=jnp.float32)
        scores = jnp.where(visible, scores * HD ** (-0.5), masked_score)
        weights, total = blended(scores, prompt_values)
        result = jnp.dot(weights.astype(jnp.bfloat16), prompt_values, preferred_element_type=jnp.float32)
        result = (result / total).astype(jnp.bfloat16)
        co_send[i * per : (i + 1) * per] = jnp.concatenate([result, out_pad], axis=1).reshape(per, tok, LANES)
    start_exchange(co_send, co_recv, co_sems)

    end_exchange(so_send, so_recv, so_sems)
    self_out_ref[0] = jnp.concatenate([so_recv[n][:, :HD].astype(jnp.float32) for n in range(HEADS)], axis=1)
    end_exchange(co_send, co_recv, co_sems)
    cross_out_ref[0] = jnp.concatenate([co_recv[n][:, :HD].astype(jnp.float32) for n in range(HEADS)], axis=1)

    for k in range(len(SUM_CUTS)):

        def drain(q, _):
            @pl.when(q > u)
            def _():
                go_up(q, k).wait_send()

            @pl.when(q < u)
            def _():
                go_down(q, k).wait_send()

            return 0

        lax.fori_loop(0, LINE, drain, 0)
    for k in cuts:
        to_half(k).wait_send()
        for i in range(1, n_x):
            x_copy(i, h, k).wait_send()
            x_copy(i, 1 - h, k).wait_send()
        for i in range(1, n_y):
            y_copy(i, k).wait_send()
        for i in range(HALF):
            spread(here, i, i, k).wait_send()
        for i in range(1, HALF):
            spread(there, i, HALF - 1 + i, k).wait_send()

        def drain_twin(g, _):
            to_other_core(c, g, k).wait_send()
            return 0

        lax.fori_loop(0, LINE, drain_twin, 0)
    drain_exchange(cq_send, cq_recv, cq_sems)
    drain_exchange(sf_send, sf_recv, sf_sems)
    drain_exchange(so_send, so_recv, so_sems)
    drain_exchange(co_send, co_recv, co_sems)


def shards(
    dims,
    image_queries,
    cross_queries,
    fresh_kv,
    stale_kv,
    prompt_states,
    caption_weight,
    cross_kv_weight,
    prompt_lengths,
    prompt_route,
):
    n_y, n_h, n_x = dims
    operands = (
        prompt_states,
        caption_weight,
        cross_kv_weight.T,
        image_queries,
        cross_queries,
        fresh_kv,
        stale_kv,
    )
    tok, width = image_queries.shape[1:]
    piece = (TILES, TILE, LANES)
    dma = pltpu.SemaphoreType.DMA
    vmem = pl.BlockSpec(memory_space=pltpu.VMEM)
    smem = pl.BlockSpec(memory_space=pltpu.SMEM)
    f32, bf16 = jnp.float32, jnp.bfloat16
    sum_lines, lines, cuts = (LINE, len(SUM_CUTS)), (LINE, len(CUTS)), len(CUTS)
    hbm = pl.BlockSpec(memory_space=pltpu.HBM)
    by_head = pltpu.VMEM((HEADS, tok, LANES), bf16)
    by_head_wide = pltpu.VMEM((HEADS, tok, 3 * LANES), bf16)
    return pl.pallas_call(
        functools.partial(kernel, dims),
        out_shape=[jax.ShapeDtypeStruct((1, tok, width), f32)] * 2,
        in_specs=[smem, smem] + [hbm] * 7,
        out_specs=[vmem, vmem],
        scratch_shapes=[
            *(pltpu.VMEM(array.shape, bf16) for array in operands),
            pltpu.VMEM((2, LINE, *piece), f32),
            pltpu.VMEM((LINE, *piece), f32),
            pltpu.VMEM((LINE, *piece), f32),
            pltpu.VMEM((LINE, *piece), f32),
            [pltpu.VMEM((n_x, n_h, m, TILE, LANES), bf16) for _, m in CUTS],
            [pltpu.VMEM((n_y, m, TILE, LANES), bf16) for _, m in CUTS],
            [pltpu.VMEM((n_y, m, TILE, LANES), bf16) for _, m in CUTS],
            pltpu.VMEM((2, LINE, *piece), bf16),
            by_head,
            by_head,
            by_head_wide,
            by_head_wide,
            by_head,
            by_head,
            by_head,
            by_head,
            dma((len(operands),)),
            dma((2,)),
            dma((2, *sum_lines)),
            dma((2, *sum_lines)),
            dma((2, cuts)),
            dma((2, cuts, n_h, n_x)),
            dma((2, cuts, n_y)),
            dma((LINE - 1, cuts)),
            dma(lines),
            dma((2, *lines)),
            dma((2, HEADS)),
            dma((2, HEADS)),
            dma((2, HEADS)),
            dma((2, HEADS)),
        ],
        compiler_params=pltpu.CompilerParams(
            collective_id=0, has_side_effects=True, vmem_limit_bytes=60 * 1024 * 1024
        ),
    )(prompt_route, prompt_lengths, *operands)


def solution(mesh, dims=(4, 2, 4)):
    in_specs = (
        P("req", "patch", None),
        P("req", "patch", None),
        P("req", "patch", None),
        P("req", "patch", None),
        P("req", None, "patch"),
        P("patch", None),
        P(None, "patch"),
        P(),
        P(),
    )
    out_specs = (P("req", "patch", None), P("req", "patch", None))
    return jax.shard_map(
        functools.partial(shards, dims), mesh=mesh, in_specs=in_specs, out_specs=out_specs, check_vma=False
    )
```

```python
import functools

import jax
import jax.numpy as jnp
from jax import lax
from jax.experimental import pallas as pl
from jax.experimental.pallas import tpu as pltpu
from jax.sharding import PartitionSpec as P

HEADS = 16
HD = 72
LANES = 128
TILE = 16
TILES = 11
LINE = 8
HALF = LINE // 2
SUM_CUTS = ((0, 3), (3, 3), (6, 3), (9, 2))
CUTS = ((0, 6), (6, 5))
masked_score = -1e30
MESH = pl.DeviceIdType.MESH


def kernel(
    dims,
    route_ref,
    lengths_ref,
    prompt_hbm,
    caption_w_hbm,
    kv_w_hbm,
    image_q_hbm,
    cross_q_hbm,
    fresh_hbm,
    stale_hbm,
    self_out_ref,
    cross_out_ref,
    prompt_ref,
    caption_w_ref,
    kv_w_ref,
    image_q_ref,
    cross_q_ref,
    fresh_ref,
    stale_ref,
    part,
    sib_part,
    running,
    crossed,
    terms,
    routed,
    y_send,
    y_recv,
    caption,
    cq_send,
    cq_recv,
    sf_send,
    sf_recv,
    so_send,
    so_recv,
    co_send,
    co_recv,
    fresh_stats,
    fresh_blend,
    load_sems,
    sib_sems,
    run_sems,
    cross_sems,
    term_sems,
    h_sems,
    x_sems,
    y_sems,
    gather_send,
    gather_recv,
    twin_sems,
    cq_sems,
    sf_sems,
    so_sems,
    co_sems,
):
    n_y, n_h, n_x = dims
    me_r = lax.axis_index("req")
    me_p = lax.axis_index("patch")
    y = me_r // (n_h * n_x)
    h = (me_r // n_x) % n_h
    x = me_r % n_x
    z = me_p // 2
    c = me_p % 2
    u = z
    shift = h * HALF

    def piece_of(pos):
        return (pos + shift) % LINE

    def patch_peer(i):
        return {"patch": (me_p + i) % (2 * LINE)}

    twin = {"patch": 2 * z + 1 - c}
    half_peer = {"req": me_r + n_x * (1 - 2 * h), "patch": 2 * ((z + HALF) % LINE) + c}

    def x_peer(i):
        return {"req": me_r - x + (x + i) % n_x}

    def y_peer(i):
        return {"req": ((y + i) % n_y) * (n_h * n_x) + h * n_x + x}

    def copy(src, dst, send, recv, device):
        return pltpu.make_async_remote_copy(
            src_ref=src, dst_ref=dst, send_sem=send, recv_sem=recv, device_id=device, device_id_type=MESH
        )

    loads = [
        pltpu.make_async_copy(src, dst, load_sems.at[i])
        for i, (src, dst) in enumerate(
            (
                (prompt_hbm, prompt_ref),
                (caption_w_hbm, caption_w_ref),
                (cross_q_hbm, cross_q_ref),
                (image_q_hbm, image_q_ref),
                (stale_hbm, stale_ref),
                (fresh_hbm, fresh_ref),
                (kv_w_hbm, kv_w_ref),
            )
        )
    ]
    barrier = pltpu.get_barrier_semaphore()
    greeted = 0
    for device in (
        [patch_peer(i) for i in range(1, 2 * LINE)]
        + [half_peer]
        + [x_peer(i) for i in range(1, n_x)]
        + [y_peer(i) for i in range(1, n_y)]
    ):
        pl.semaphore_signal(barrier, inc=1, device_id=device, device_id_type=MESH)
        greeted += 1
    for load in loads:
        load.start()

    loads[0].wait()
    loads[1].wait()
    prompt = prompt_ref[0]
    rows = prompt.shape[0]
    row_tiles = -(-rows // TILE)
    prompt = jnp.concatenate(
        [prompt, jnp.zeros((row_tiles * TILE - rows, prompt.shape[1]), prompt.dtype)], axis=0
    )
    width = caption_w_ref.shape[1]
    col_tiles = width // LANES

    def place(i, j):
        piece, at = divmod(i * col_tiles + j, TILES)
        return piece // LINE, piece % LINE, at

    slots = [piece_of(g) for g in range(LINE)]

    group = 3
    for j0 in range(0, col_tiles, group):
        block = jnp.dot(
            prompt, caption_w_ref[:, j0 * LANES : (j0 + group) * LANES], preferred_element_type=jnp.float32
        )
        for i in range(row_tiles):
            for j in range(group):
                core, g, at = place(i, j0 + j)
                part[core, slots[g], at] = block[i * TILE : (i + 1) * TILE, j * LANES : (j + 1) * LANES]
    for t in range(row_tiles * col_tiles, 2 * LINE * TILES):
        part[t // (LINE * TILES), slots[(t // TILES) % LINE], t % TILES] = jnp.zeros((TILE, LANES), jnp.float32)

    to_twin = copy(part.at[1 - c], sib_part, sib_sems.at[0], sib_sems.at[1], twin)
    pl.semaphore_wait(barrier, greeted)
    to_twin.start()
    for load in loads[2:]:
        load.wait()

    tok = image_q_ref.shape[1]
    pad_c = jnp.zeros((tok, LANES - HD), jnp.bfloat16)
    pad_s = jnp.zeros((tok, 2 * LANES - 3 * HD), jnp.bfloat16)
    for n in range(HEADS):
        a, b = n * HD, (n + 1) * HD
        cq_send[n] = jnp.concatenate([cross_q_ref[0, :, a:b], pad_c], axis=1)
        sf_send[n] = jnp.concatenate(
            [
                image_q_ref[0, :, a:b],
                stale_ref[0, :, a:b],
                stale_ref[0, :, width + a : width + b],
                pad_s,
            ],
            axis=1,
        )

    def exchange(send, recv, sems, i):
        peer = (me_p + i) % (2 * LINE)
        return copy(send.at[peer], recv.at[me_p], sems.at[0, i], sems.at[1, i], {"patch": peer})

    def arrival(send, recv, sems, i):
        origin = (me_p - i + 2 * LINE) % (2 * LINE)
        return copy(send.at[origin], recv.at[origin], sems.at[0, i], sems.at[1, i], {"patch": origin})

    def start_exchange(send, recv, sems):
        recv[me_p] = send[me_p]

        def step(i, _):
            exchange(send, recv, sems, i).start()
            return 0

        lax.fori_loop(1, 2 * LINE, step, 0)

    def end_exchange(send, recv, sems):
        def step(i, _):
            arrival(send, recv, sems, i).wait_recv()
            return 0

        lax.fori_loop(1, 2 * LINE, step, 0)

    def drain_exchange(send, recv, sems):
        def step(i, _):
            exchange(send, recv, sems, i).wait_send()
            return 0

        lax.fori_loop(1, 2 * LINE, step, 0)

    start_exchange(cq_send, cq_recv, cq_sems)
    to_twin.wait_recv()
    to_twin.wait_send()
    sums = part.at[c]

    def add_twin(i, _):
        sums[i] = sums[i] + sib_part[i]
        return 0

    lax.fori_loop(0, LINE, add_twin, 0)

    inner = HALF - 1
    left = u < HALF
    deep = jnp.where(left, u, LINE - 1 - u)

    def at(pos):
        return jnp.where(left, pos, LINE - 1 - pos)

    def at_device(pos):
        return {"patch": 2 * at(pos) + c}

    def sum_cut(k):
        a, m = SUM_CUTS[k]
        return pl.ds(a, m)

    def inward(pos, k):
        return copy(
            sums.at[at(pos), sum_cut(k)],
            running.at[at(pos), sum_cut(k)],
            run_sems.at[0, pos, k],
            run_sems.at[1, pos, k],
            at_device(jnp.minimum(deep + 1, inner)),
        )

    def across(pos, k):
        return copy(
            sums.at[at(pos), sum_cut(k)],
            crossed.at[sum_cut(k)],
            cross_sems.at[0, pos, k],
            cross_sems.at[1, 0, k],
            at_device(pos),
        )

    def outward(pos):
        return copy(
            sums.at[at(pos)], terms.at[deep], term_sems.at[0, pos], term_sems.at[1, deep], at_device(pos)
        )

    def term_arrival(pos):
        return copy(sums.at[u], terms.at[pos], term_sems.at[0, 0], term_sems.at[1, pos], at_device(pos))

    for pos in range(inner):

        @pl.when(pos < deep)
        def _():
            outward(pos).start()

    def reduce_step(t, _):
        pos = LINE - 1 - t

        @pl.when(pos >= deep)
        def _():
            for k in range(len(SUM_CUTS)):

                @pl.when(deep > 0)
                def _():
                    inward(pos, k).wait_recv()
                    sums[at(pos), sum_cut(k)] = sums[at(pos), sum_cut(k)] + running[at(pos), sum_cut(k)]

                @pl.when((pos > deep) & (deep < inner))
                def _():
                    inward(pos, k).start()

                @pl.when((pos > deep) & (deep == inner))
                def _():
                    across(pos, k).start()

        return 0

    lax.fori_loop(0, LINE, reduce_step, 0)
    for pos in range(1, HALF):

        @pl.when(pos > deep)
        def _():
            term_arrival(pos).wait_recv()
            sums[u] = sums[u] + terms[pos]

    for k in range(len(SUM_CUTS)):
        across(inner + 1, k).wait_recv()

    def to_half(k):
        ref = routed[k].at[x, h]
        return copy(ref, ref, h_sems.at[0, k], h_sems.at[1, k], half_peer)

    def half_arrival(k):
        ref = routed[k].at[x, 1 - h]
        return copy(ref, ref, h_sems.at[0, k], h_sems.at[1, k], half_peer)

    def x_copy(i, half, k):
        ref = routed[k].at[x, half]
        return copy(ref, ref, x_sems.at[0, k, half, i], x_sems.at[1, k, half, i], x_peer(i))

    def x_arrival(i, half, k):
        ref = routed[k].at[(x - i + n_x) % n_x, half]
        return copy(ref, ref, x_sems.at[0, k, half, i], x_sems.at[1, k, half, i], x_peer(i))

    def wanted(i, k):
        source = route_ref[((y + i) % n_y) * (n_h * n_x) + h * n_x + x]
        return routed[k][lax.rem(source, n_x), lax.rem(lax.div(source, n_x), n_h)]

    def y_copy(i, k):
        return copy(y_send[k].at[i], y_recv[k].at[y], y_sems.at[0, k, i], y_sems.at[1, k, i], y_peer(i))

    def y_arrival(i, k):
        ref = y_recv[k].at[(y - i + n_y) % n_y]
        return copy(ref, ref, y_sems.at[0, k, i], y_sems.at[1, k, i], y_peer(i))

    here = piece_of(u)
    there = piece_of((u + HALF) % LINE)

    def beside(i):
        return (u // HALF) * HALF + (u + i) % HALF

    def tiles_of(core, g, k):
        a, m = CUTS[k]
        return caption.at[core, g, pl.ds(a, m)]

    def spread(g, i, n, k):
        pos = beside(i) if i else (u + HALF) % LINE
        ref = tiles_of(c, g, k)
        return copy(ref, ref, gather_send.at[n, k], gather_recv.at[g, k], {"patch": 2 * pos + c})

    def gathered(g, k):
        ref = tiles_of(c, g, k)
        return copy(ref, ref, gather_send.at[0, k], gather_recv.at[g, k], twin)

    def to_other_core(core, g, k):
        ref = tiles_of(core, g, k)
        return copy(ref, ref, twin_sems.at[0, g, k], twin_sems.at[1, g, k], twin)

    cuts = range(len(CUTS))
    for k, (a, m) in enumerate(CUTS):
        piece = sums[u, a : a + m] + crossed[a : a + m]
        piece = jax.nn.gelu(piece, approximate=True).astype(jnp.bfloat16)
        routed[k][x, h] = piece
        to_half(k).start()
        for i in range(1, n_x):
            x_copy(i, h, k).start()
    start_exchange(sf_send, sf_recv, sf_sems)

    seq = 2 * LINE * tok
    contract_last = (((1,), (1,)), ((), ()))
    chunk = LANES
    per = chunk // tok
    zero = jnp.zeros((), jnp.bfloat16)
    head_of = lax.broadcasted_iota(jnp.int32, (tok, width), 1) // HD

    def apart(rows):
        return jnp.concatenate([jnp.where(head_of == n, rows, zero) for n in range(HEADS)], axis=0)

    fresh_scores = lax.dot_general(
        apart(image_q_ref[0]), fresh_ref[0, :, :width], contract_last, preferred_element_type=jnp.float32
    )
    fresh_scores = fresh_scores * HD ** (-0.5)
    fresh_base = jnp.max(fresh_scores, axis=-1, keepdims=True)
    fresh_weights = jnp.exp(fresh_scores - fresh_base)
    fresh_total = jnp.sum(fresh_weights, axis=-1, keepdims=True)
    fresh_weights = fresh_weights.astype(jnp.bfloat16)
    fresh_stats[:, 0:1] = fresh_base
    fresh_stats[:, 1:2] = fresh_total
    fresh_blend[...] = jnp.dot(
        jnp.concatenate([fresh_weights[n * tok : (n + 1) * tok] for n in range(HEADS)], axis=1),
        apart(fresh_ref[0, :, width:]),
        preferred_element_type=jnp.float32,
    )

    for k in cuts:
        half_arrival(k).wait_recv()
        for i in range(1, n_x):
            x_copy(i, 1 - h, k).start()
    for k in cuts:
        for i in range(1, n_x):
            x_arrival(i, h, k).wait_recv()
            x_arrival(i, 1 - h, k).wait_recv()
        for i in range(1, n_y):
            y_send[k][i] = wanted(i, k)
            y_copy(i, k).start()
        y_recv[k][y] = wanted(0, k)
    source = route_ref[me_r]
    for k, (a, m) in enumerate(CUTS):
        for i in range(1, n_y):
            y_arrival(i, k).wait_recv()
        caption[c, here, a : a + m] = y_recv[k][lax.div(source, n_h * n_x)]
        for i in range(HALF):
            spread(here, i, i, k).start()
        to_other_core(c, here, k).start()

    end_exchange(sf_send, sf_recv, sf_sems)
    whole = sf_recv[...].reshape(seq, 2 * LANES)
    queries, keys, values = whole[:, :HD], whole[:, HD : 2 * HD], whole[:, 2 * HD : 3 * HD]
    own = (
        lax.broadcasted_iota(jnp.int32, (chunk, chunk), 0) // tok
        == lax.broadcasted_iota(jnp.int32, (chunk, chunk), 1) // tok
    )
    self_pad = jnp.zeros((chunk, LANES - HD - 3), jnp.bfloat16)
    for i in range(seq // chunk):
        a, b = i * chunk, (i + 1) * chunk
        scores = lax.dot_general(queries[a:b], keys, contract_last, preferred_element_type=jnp.float32)
        scores = scores * HD ** (-0.5)
        mixed = [jnp.where(own, masked_score, scores[:, a:b])]
        if a > 0:
            mixed = [scores[:, :a]] + mixed
        if b < seq:
            mixed = mixed + [scores[:, b:]]
        scores = jnp.concatenate(mixed, axis=1)
        base = jnp.max(scores, axis=-1, keepdims=True).astype(jnp.bfloat16)
        weights = jnp.exp(scores - base.astype(jnp.float32))
        total = jnp.sum(weights, axis=-1, keepdims=True)
        result = jnp.dot(weights.astype(jnp.bfloat16), values, preferred_element_type=jnp.float32)
        result = (result / total).astype(jnp.bfloat16)
        total_high = total.astype(jnp.bfloat16)
        total_low = (total - total_high.astype(jnp.float32)).astype(jnp.bfloat16)
        so_send[i * per : (i + 1) * per] = jnp.concatenate(
            [result, base, total_high, total_low, self_pad], axis=1
        ).reshape(per, tok, LANES)
    start_exchange(so_send, so_recv, so_sems)

    for k in cuts:
        gathered(there, k).wait_recv()
        for i in range(1, HALF):
            spread(there, i, HALF - 1 + i, k).start()
        to_other_core(c, there, k).start()
    for far in (0, HALF):
        for k in cuts:
            for i in range(1, HALF):
                g = piece_of((beside(i) + far) % LINE)
                gathered(g, k).wait_recv()
                to_other_core(c, g, k).start()

    end_exchange(cq_send, cq_recv, cq_sems)

    def twin_wait(q, _):
        for k in range(len(CUTS)):
            to_other_core(1 - c, q, k).wait_recv()
        return 0

    lax.fori_loop(0, LINE, twin_wait, 0)
    caption_rows = jnp.concatenate(
        [jnp.concatenate([caption[place(i, j)] for j in range(col_tiles)], axis=1) for i in range(row_tiles)], axis=0
    )
    head_states = lax.dot_general(
        caption_rows, kv_w_ref[...], contract_last, preferred_element_type=jnp.float32
    ).astype(jnp.bfloat16)
    prompt_keys, prompt_values = head_states[:, :HD], head_states[:, HD : 2 * HD]
    out_pad = jnp.zeros((chunk, LANES - HD), jnp.bfloat16)
    length = lengths_ref[source]
    visible = lax.broadcasted_iota(jnp.int32, (1, row_tiles * TILE), 1) < length
    cross_rows = cq_recv[...].reshape(seq, LANES)[:, :HD]
    for i in range(seq // chunk):
        a, b = i * chunk, (i + 1) * chunk
        scores = lax.dot_general(cross_rows[a:b], prompt_keys, contract_last, preferred_element_type=jnp.float32)
        scores = jnp.where(visible, scores * HD ** (-0.5), masked_score)
        weights = jnp.exp(scores - jnp.max(scores, axis=-1, keepdims=True))
        total = jnp.sum(weights, axis=-1, keepdims=True)
        result = jnp.dot(weights.astype(jnp.bfloat16), prompt_values, preferred_element_type=jnp.float32)
        result = (result / total).astype(jnp.bfloat16)
        co_send[i * per : (i + 1) * per] = jnp.concatenate([result, out_pad], axis=1).reshape(per, tok, LANES)
    start_exchange(co_send, co_recv, co_sems)

    end_exchange(so_send, so_recv, so_sems)
    merged = []
    for n in range(HEADS):
        block = so_recv[n].astype(jnp.float32)
        stale_base = block[:, HD : HD + 1]
        stale_total = block[:, HD + 1 : HD + 2] + block[:, HD + 2 : HD + 3]
        own_base = fresh_stats[n * tok : (n + 1) * tok, 0:1]
        own_total = fresh_stats[n * tok : (n + 1) * tok, 1:2]
        top = jnp.maximum(stale_base, own_base)
        stale_share = stale_total * jnp.exp(stale_base - top)
        own_scale = jnp.exp(own_base - top)
        both = stale_share + own_total * own_scale
        merged.append(
            block[:, :HD] * (stale_share / both) + fresh_blend[:, n * HD : (n + 1) * HD] * (own_scale / both)
        )
    self_out_ref[0] = jnp.concatenate(merged, axis=1)
    end_exchange(co_send, co_recv, co_sems)
    cross_out_ref[0] = jnp.concatenate([co_recv[n][:, :HD].astype(jnp.float32) for n in range(HEADS)], axis=1)

    for pos in range(inner):

        @pl.when(pos < deep)
        def _():
            outward(pos).wait_send()

    def drain(pos, _):
        for k in range(len(SUM_CUTS)):

            @pl.when((pos > deep) & (deep < inner))
            def _():
                inward(pos, k).wait_send()

            @pl.when((pos > deep) & (deep == inner))
            def _():
                across(pos, k).wait_send()

        return 0

    lax.fori_loop(0, LINE, drain, 0)
    for k in cuts:
        to_half(k).wait_send()
        for i in range(1, n_x):
            x_copy(i, h, k).wait_send()
            x_copy(i, 1 - h, k).wait_send()
        for i in range(1, n_y):
            y_copy(i, k).wait_send()
        for i in range(HALF):
            spread(here, i, i, k).wait_send()
        for i in range(1, HALF):
            spread(there, i, HALF - 1 + i, k).wait_send()

        def drain_twin(g, _):
            to_other_core(c, g, k).wait_send()
            return 0

        lax.fori_loop(0, LINE, drain_twin, 0)
    drain_exchange(cq_send, cq_recv, cq_sems)
    drain_exchange(sf_send, sf_recv, sf_sems)
    drain_exchange(so_send, so_recv, so_sems)
    drain_exchange(co_send, co_recv, co_sems)


def shards(
    dims,
    image_queries,
    cross_queries,
    fresh_kv,
    stale_kv,
    prompt_states,
    caption_weight,
    cross_kv_weight,
    prompt_lengths,
    prompt_route,
):
    n_y, n_h, n_x = dims
    operands = (
        prompt_states,
        caption_weight,
        cross_kv_weight.T,
        image_queries,
        cross_queries,
        fresh_kv,
        stale_kv,
    )
    tok, width = image_queries.shape[1:]
    piece = (TILES, TILE, LANES)
    dma = pltpu.SemaphoreType.DMA
    vmem = pl.BlockSpec(memory_space=pltpu.VMEM)
    smem = pl.BlockSpec(memory_space=pltpu.SMEM)
    f32, bf16 = jnp.float32, jnp.bfloat16
    sum_lines, lines, cuts = (LINE, len(SUM_CUTS)), (LINE, len(CUTS)), len(CUTS)
    hbm = pl.BlockSpec(memory_space=pltpu.HBM)
    by_head = pltpu.VMEM((HEADS, tok, LANES), bf16)
    by_head_wide = pltpu.VMEM((HEADS, tok, 2 * LANES), bf16)
    return pl.pallas_call(
        functools.partial(kernel, dims),
        out_shape=[jax.ShapeDtypeStruct((1, tok, width), f32)] * 2,
        in_specs=[smem, smem] + [hbm] * 7,
        out_specs=[vmem, vmem],
        scratch_shapes=[
            *(pltpu.VMEM(array.shape, bf16) for array in operands),
            pltpu.VMEM((2, LINE, *piece), f32),
            pltpu.VMEM((LINE, *piece), f32),
            pltpu.VMEM((LINE, *piece), f32),
            pltpu.VMEM(piece, f32),
            pltpu.VMEM((HALF, *piece), f32),
            [pltpu.VMEM((n_x, n_h, m, TILE, LANES), bf16) for _, m in CUTS],
            [pltpu.VMEM((n_y, m, TILE, LANES), bf16) for _, m in CUTS],
            [pltpu.VMEM((n_y, m, TILE, LANES), bf16) for _, m in CUTS],
            pltpu.VMEM((2, LINE, *piece), bf16),
            by_head,
            by_head,
            by_head_wide,
            by_head_wide,
            by_head,
            by_head,
            by_head,
            by_head,
            pltpu.VMEM((HEADS * tok, LANES), f32),
            pltpu.VMEM((tok, width), f32),
            dma((len(operands),)),
            dma((2,)),
            dma((2, *sum_lines)),
            dma((2, *sum_lines)),
            dma((2, HALF)),
            dma((2, cuts)),
            dma((2, cuts, n_h, n_x)),
            dma((2, cuts, n_y)),
            dma((LINE - 1, cuts)),
            dma(lines),
            dma((2, *lines)),
            dma((2, HEADS)),
            dma((2, HEADS)),
            dma((2, HEADS)),
            dma((2, HEADS)),
        ],
        compiler_params=pltpu.CompilerParams(
            collective_id=0, has_side_effects=True, vmem_limit_bytes=56 * 1024 * 1024
        ),
    )(prompt_route, prompt_lengths, *operands)


def solution(mesh, dims=(4, 2, 4)):
    in_specs = (
        P("req", "patch", None),
        P("req", "patch", None),
        P("req", "patch", None),
        P("req", "patch", None),
        P("req", None, "patch"),
        P("patch", None),
        P(None, "patch"),
        P(),
        P(),
    )
    out_specs = (P("req", "patch", None), P("req", "patch", None))
    return jax.shard_map(
        functools.partial(shards, dims), mesh=mesh, in_specs=in_specs, out_specs=out_specs, check_vma=False
    )
```

```python
import functools

import jax
import jax.numpy as jnp
from jax import lax
from jax.experimental import pallas as pl
from jax.experimental.pallas import tpu as pltpu
from jax.sharding import PartitionSpec as P

HEADS = 16
HD = 72
LANES = 128
TILE = 16
TILES = 11
LINE = 8
HALF = LINE // 2
masked_score = -1e30
MESH = pl.DeviceIdType.MESH
SUM_CUTS = ((0, 3), (3, 3), (6, 3), (9, 2))
CUTS = ((0, 6), (6, 5))


def kernel(
    dims,
    route_ref,
    lengths_ref,
    prompt_hbm,
    caption_w_hbm,
    kv_w_hbm,
    image_q_hbm,
    cross_q_hbm,
    fresh_hbm,
    stale_hbm,
    self_out_ref,
    cross_out_ref,
    prompt_ref,
    caption_w_ref,
    kv_w_ref,
    image_q_ref,
    cross_q_ref,
    fresh_ref,
    stale_ref,
    part,
    sib_part,
    running,
    crossed,
    terms,
    routed,
    y_send,
    y_recv,
    caption,
    cq_send,
    cq_recv,
    sf_send,
    sf_recv,
    so_send,
    so_recv,
    co_send,
    co_recv,
    fresh_stats,
    fresh_blend,
    load_sems,
    sib_sems,
    run_sems,
    cross_sems,
    term_sems,
    h_sems,
    x_sems,
    y_sems,
    gather_send,
    gather_recv,
    twin_sems,
    cq_sems,
    sf_sems,
    so_sems,
    co_sems,
):
    n_y, n_h, n_x = dims
    me_r = lax.axis_index("req")
    me_p = lax.axis_index("patch")
    y = me_r // (n_h * n_x)
    h = (me_r // n_x) % n_h
    x = me_r % n_x
    z = me_p // 2
    c = me_p % 2
    u = z
    shift = h * HALF

    def piece_of(pos):
        return (pos + shift) % LINE

    def patch_peer(i):
        return {"patch": (me_p + i) % (2 * LINE)}

    twin = {"patch": 2 * z + 1 - c}
    half_peer = {"req": me_r + n_x * (1 - 2 * h), "patch": 2 * ((z + HALF) % LINE) + c}

    def x_peer(i):
        return {"req": me_r - x + (x + i) % n_x}

    def y_peer(i):
        return {"req": ((y + i) % n_y) * (n_h * n_x) + h * n_x + x}

    def copy(src, dst, send, recv, device):
        return pltpu.make_async_remote_copy(
            src_ref=src, dst_ref=dst, send_sem=send, recv_sem=recv, device_id=device, device_id_type=MESH
        )

    loads = [
        pltpu.make_async_copy(src, dst, load_sems.at[i])
        for i, (src, dst) in enumerate(
            (
                (prompt_hbm, prompt_ref),
                (caption_w_hbm, caption_w_ref),
                (cross_q_hbm, cross_q_ref),
                (image_q_hbm, image_q_ref),
                (stale_hbm, stale_ref),
                (fresh_hbm, fresh_ref),
                (kv_w_hbm, kv_w_ref),
            )
        )
    ]
    barrier = pltpu.get_barrier_semaphore()
    greeted = 0
    for device in (
        [patch_peer(i) for i in range(1, 2 * LINE)]
        + [half_peer]
        + [x_peer(i) for i in range(1, n_x)]
        + [y_peer(i) for i in range(1, n_y)]
    ):
        pl.semaphore_signal(barrier, inc=1, device_id=device, device_id_type=MESH)
        greeted += 1
    for load in loads:
        load.start()

    loads[0].wait()
    loads[1].wait()
    prompt = prompt_ref[0]
    rows = prompt.shape[0]
    row_tiles = -(-rows // TILE)
    prompt = jnp.concatenate(
        [prompt, jnp.zeros((row_tiles * TILE - rows, prompt.shape[1]), prompt.dtype)], axis=0
    )
    width = caption_w_ref.shape[1]
    col_tiles = width // LANES

    def place(i, j):
        piece, at = divmod(i * col_tiles + j, TILES)
        return piece // LINE, piece % LINE, at

    slots = [piece_of(g) for g in range(LINE)]

    group = 3
    for j0 in range(0, col_tiles, group):
        block = jnp.dot(
            prompt, caption_w_ref[:, j0 * LANES : (j0 + group) * LANES], preferred_element_type=jnp.float32
        )
        for i in range(row_tiles):
            for j in range(group):
                core, g, at = place(i, j0 + j)
                part[core, slots[g], at] = block[i * TILE : (i + 1) * TILE, j * LANES : (j + 1) * LANES]
    for t in range(row_tiles * col_tiles, 2 * LINE * TILES):
        part[t // (LINE * TILES), slots[(t // TILES) % LINE], t % TILES] = jnp.zeros((TILE, LANES), jnp.float32)

    left = u < HALF
    deep = jnp.where(left, u, LINE - 1 - u)

    def at(pos):
        return jnp.where(left, pos, LINE - 1 - pos)

    def to_twin(pos):
        return copy(part.at[1 - c, at(pos)], sib_part.at[at(pos)], sib_sems.at[0, pos], sib_sems.at[1, pos], twin)

    pl.semaphore_wait(barrier, greeted)
    for pos in reversed(range(LINE)):
        to_twin(pos).start()
    for load in loads[2:]:
        load.wait()

    tok = image_q_ref.shape[1]
    pad_c = jnp.zeros((tok, LANES - HD), jnp.bfloat16)
    pad_s = jnp.zeros((tok, 2 * LANES - 3 * HD), jnp.bfloat16)
    for n in range(HEADS):
        a, b = n * HD, (n + 1) * HD
        cq_send[n] = jnp.concatenate([cross_q_ref[0, :, a:b], pad_c], axis=1)
        sf_send[n] = jnp.concatenate(
            [
                image_q_ref[0, :, a:b],
                stale_ref[0, :, a:b],
                stale_ref[0, :, width + a : width + b],
                pad_s,
            ],
            axis=1,
        )

    def exchange(send, recv, sems, i):
        peer = (me_p + i) % (2 * LINE)
        return copy(send.at[peer], recv.at[me_p], sems.at[0, i], sems.at[1, i], {"patch": peer})

    def arrival(send, recv, sems, i):
        origin = (me_p - i + 2 * LINE) % (2 * LINE)
        return copy(send.at[origin], recv.at[origin], sems.at[0, i], sems.at[1, i], {"patch": origin})

    def start_exchange(send, recv, sems):
        recv[me_p] = send[me_p]

        def step(i, _):
            exchange(send, recv, sems, i).start()
            return 0

        lax.fori_loop(1, 2 * LINE, step, 0)

    def start_some(send, recv, sems, first, count):
        def step(n, _):
            @pl.when(n == me_p)
            def _():
                recv[n] = send[n]

            @pl.when(n != me_p)
            def _():
                exchange(send, recv, sems, (n - me_p + 2 * LINE) % (2 * LINE)).start()

            return 0

        lax.fori_loop(first, first + count, step, 0)

    def end_exchange(send, recv, sems):
        def step(i, _):
            arrival(send, recv, sems, i).wait_recv()
            return 0

        lax.fori_loop(1, 2 * LINE, step, 0)

    def drain_exchange(send, recv, sems):
        def step(i, _):
            exchange(send, recv, sems, i).wait_send()
            return 0

        lax.fori_loop(1, 2 * LINE, step, 0)

    start_exchange(cq_send, cq_recv, cq_sems)
    sums = part.at[c]

    def add_twin(pos):
        to_twin(pos).wait_recv()
        sums[at(pos)] = sums[at(pos)] + sib_part[at(pos)]

    inner = HALF - 1
    def at_device(pos):
        return {"patch": 2 * at(pos) + c}

    def sum_cut(k):
        a, m = SUM_CUTS[k]
        return pl.ds(a, m)

    def inward(pos, k):
        return copy(
            sums.at[at(pos), sum_cut(k)],
            running.at[at(pos), sum_cut(k)],
            run_sems.at[0, pos, k],
            run_sems.at[1, pos, k],
            at_device(jnp.minimum(deep + 1, inner)),
        )

    def across(pos, k):
        return copy(
            sums.at[at(pos), sum_cut(k)],
            crossed.at[sum_cut(k)],
            cross_sems.at[0, pos, k],
            cross_sems.at[1, 0, k],
            at_device(pos),
        )

    def outward(pos):
        return copy(
            sums.at[at(pos)], terms.at[deep], term_sems.at[0, pos], term_sems.at[1, deep], at_device(pos)
        )

    def term_arrival(pos):
        return copy(sums.at[u], terms.at[pos], term_sems.at[0, 0], term_sems.at[1, pos], at_device(pos))

    def first_step(t, _):
        pos = LINE - 1 - t
        add_twin(pos)

        @pl.when(pos < deep)
        def _():
            outward(pos).start()

        return 0

    @pl.when(deep > 0)
    def _():
        lax.fori_loop(0, LINE, first_step, 0)

    def reduce_step(t, _):
        pos = LINE - 1 - t

        @pl.when(deep == 0)
        def _():
            add_twin(pos)

        @pl.when(pos >= deep)
        def _():
            for k in range(len(SUM_CUTS)):

                @pl.when(deep > 0)
                def _():
                    inward(pos, k).wait_recv()
                    sums[at(pos), sum_cut(k)] = sums[at(pos), sum_cut(k)] + running[at(pos), sum_cut(k)]

                @pl.when((pos > deep) & (deep < inner))
                def _():
                    inward(pos, k).start()

                @pl.when((pos > deep) & (deep == inner))
                def _():
                    across(pos, k).start()

        return 0

    lax.fori_loop(0, LINE, reduce_step, 0)
    for pos in range(1, HALF):

        @pl.when(pos > deep)
        def _():
            term_arrival(pos).wait_recv()
            sums[u] = sums[u] + terms[pos]

    for k in range(len(SUM_CUTS)):
        across(inner + 1, k).wait_recv()

    def to_half(k):
        ref = routed[k].at[x, h]
        return copy(ref, ref, h_sems.at[0, k], h_sems.at[1, k], half_peer)

    def half_arrival(k):
        ref = routed[k].at[x, 1 - h]
        return copy(ref, ref, h_sems.at[0, k], h_sems.at[1, k], half_peer)

    def x_copy(i, half, k):
        ref = routed[k].at[x, half]
        return copy(ref, ref, x_sems.at[0, k, half, i], x_sems.at[1, k, half, i], x_peer(i))

    def x_arrival(i, half, k):
        ref = routed[k].at[(x - i + n_x) % n_x, half]
        return copy(ref, ref, x_sems.at[0, k, half, i], x_sems.at[1, k, half, i], x_peer(i))

    def wanted(i, k):
        source = route_ref[((y + i) % n_y) * (n_h * n_x) + h * n_x + x]
        return routed[k][lax.rem(source, n_x), lax.rem(lax.div(source, n_x), n_h)]

    def y_copy(i, k):
        return copy(y_send[k].at[i], y_recv[k].at[y], y_sems.at[0, k, i], y_sems.at[1, k, i], y_peer(i))

    def y_arrival(i, k):
        ref = y_recv[k].at[(y - i + n_y) % n_y]
        return copy(ref, ref, y_sems.at[0, k, i], y_sems.at[1, k, i], y_peer(i))

    here = piece_of(u)
    there = piece_of((u + HALF) % LINE)

    def beside(i):
        return (u // HALF) * HALF + (u + i) % HALF

    def tiles_of(core, g, k):
        a, m = CUTS[k]
        return caption.at[core, g, pl.ds(a, m)]

    def spread(g, i, n, k):
        pos = beside(i) if i else (u + HALF) % LINE
        ref = tiles_of(c, g, k)
        return copy(ref, ref, gather_send.at[n, k], gather_recv.at[g, k], {"patch": 2 * pos + c})

    def gathered(g, k):
        ref = tiles_of(c, g, k)
        return copy(ref, ref, gather_send.at[0, k], gather_recv.at[g, k], twin)

    def to_other_core(core, g, k):
        ref = tiles_of(core, g, k)
        return copy(ref, ref, twin_sems.at[0, g, k], twin_sems.at[1, g, k], twin)

    cuts = range(len(CUTS))
    for k, (a, m) in enumerate(CUTS):
        piece = sums[u, a : a + m] + crossed[a : a + m]
        piece = jax.nn.gelu(piece, approximate=True).astype(jnp.bfloat16)
        routed[k][x, h] = piece
        to_half(k).start()
        for i in range(1, n_x):
            x_copy(i, h, k).start()
    seq = 2 * LINE * tok
    contract_last = (((1,), (1,)), ((), ()))
    chunk = LANES
    per = chunk // tok
    zero = jnp.zeros((), jnp.bfloat16)
    head_of = lax.broadcasted_iota(jnp.int32, (tok, width), 1) // HD

    def apart(rows):
        return jnp.concatenate([jnp.where(head_of == n, rows, zero) for n in range(HEADS)], axis=0)

    fresh_scores = lax.dot_general(
        apart(image_q_ref[0]), fresh_ref[0, :, :width], contract_last, preferred_element_type=jnp.float32
    )
    fresh_scores = fresh_scores * HD ** (-0.5)
    fresh_base = jnp.max(fresh_scores, axis=-1, keepdims=True)
    fresh_weights = jnp.exp(fresh_scores - fresh_base)
    fresh_total = jnp.sum(fresh_weights, axis=-1, keepdims=True)
    fresh_weights = fresh_weights.astype(jnp.bfloat16)
    fresh_stats[:, 0:1] = fresh_base
    fresh_stats[:, 1:2] = fresh_total
    fresh_blend[...] = jnp.dot(
        jnp.concatenate([fresh_weights[n * tok : (n + 1) * tok] for n in range(HEADS)], axis=1),
        apart(fresh_ref[0, :, width:]),
        preferred_element_type=jnp.float32,
    )

    for k in cuts:
        half_arrival(k).wait_recv()
        for i in range(1, n_x):
            x_copy(i, 1 - h, k).start()
    start_exchange(sf_send, sf_recv, sf_sems)
    for k in cuts:
        for i in range(1, n_x):
            x_arrival(i, h, k).wait_recv()
            x_arrival(i, 1 - h, k).wait_recv()
        for i in range(1, n_y):
            y_send[k][i] = wanted(i, k)
            y_copy(i, k).start()
        y_recv[k][y] = wanted(0, k)
    source = route_ref[me_r]
    for k, (a, m) in enumerate(CUTS):
        for i in range(1, n_y):
            y_arrival(i, k).wait_recv()
        caption[c, here, a : a + m] = y_recv[k][lax.div(source, n_h * n_x)]
        for i in range(HALF):
            spread(here, i, i, k).start()
        to_other_core(c, here, k).start()

    for k in cuts:
        gathered(there, k).wait_recv()
        for i in range(1, HALF):
            spread(there, i, HALF - 1 + i, k).start()
        to_other_core(c, there, k).start()
    end_exchange(sf_send, sf_recv, sf_sems)
    whole = sf_recv[...].reshape(seq, 2 * LANES)
    queries, keys, values = whole[:, :HD], whole[:, HD : 2 * HD], whole[:, 2 * HD : 3 * HD]
    own = (
        lax.broadcasted_iota(jnp.int32, (chunk, chunk), 0) // tok
        == lax.broadcasted_iota(jnp.int32, (chunk, chunk), 1) // tok
    )
    self_pad = jnp.zeros((chunk, LANES - HD - 3), jnp.bfloat16)
    for i in range(seq // chunk):
        a, b = i * chunk, (i + 1) * chunk
        scores = lax.dot_general(queries[a:b], keys, contract_last, preferred_element_type=jnp.float32)
        scores = scores * HD ** (-0.5)
        mixed = [jnp.where(own, masked_score, scores[:, a:b])]
        if a > 0:
            mixed = [scores[:, :a]] + mixed
        if b < seq:
            mixed = mixed + [scores[:, b:]]
        scores = jnp.concatenate(mixed, axis=1)
        base = jnp.max(scores, axis=-1, keepdims=True).astype(jnp.bfloat16)
        weights = jnp.exp(scores - base.astype(jnp.float32))
        total = jnp.sum(weights, axis=-1, keepdims=True)
        result = jnp.dot(weights.astype(jnp.bfloat16), values, preferred_element_type=jnp.float32)
        result = (result / total).astype(jnp.bfloat16)
        total_high = total.astype(jnp.bfloat16)
        total_low = (total - total_high.astype(jnp.float32)).astype(jnp.bfloat16)
        so_send[i * per : (i + 1) * per] = jnp.concatenate(
            [result, base, total_high, total_low, self_pad], axis=1
        ).reshape(per, tok, LANES)
        start_some(so_send, so_recv, so_sems, i * per, per)

    for far in (0, HALF):
        for k in cuts:
            for i in range(1, HALF):
                g = piece_of((beside(i) + far) % LINE)
                gathered(g, k).wait_recv()
                to_other_core(c, g, k).start()

    end_exchange(cq_send, cq_recv, cq_sems)

    def twin_wait(q, _):
        for k in range(len(CUTS)):
            to_other_core(1 - c, q, k).wait_recv()
        return 0

    lax.fori_loop(0, LINE, twin_wait, 0)
    caption_rows = jnp.concatenate(
        [jnp.concatenate([caption[place(i, j)] for j in range(col_tiles)], axis=1) for i in range(row_tiles)], axis=0
    )
    head_states = lax.dot_general(
        caption_rows, kv_w_ref[...], contract_last, preferred_element_type=jnp.float32
    ).astype(jnp.bfloat16)
    prompt_keys, prompt_values = head_states[:, :HD], head_states[:, HD : 2 * HD]
    out_pad = jnp.zeros((chunk, LANES - HD), jnp.bfloat16)
    length = lengths_ref[source]
    visible = lax.broadcasted_iota(jnp.int32, (1, row_tiles * TILE), 1) < length
    cross_rows = cq_recv[...].reshape(seq, LANES)[:, :HD]
    for i in range(seq // chunk):
        a, b = i * chunk, (i + 1) * chunk
        scores = lax.dot_general(cross_rows[a:b], prompt_keys, contract_last, preferred_element_type=jnp.float32)
        scores = jnp.where(visible, scores * HD ** (-0.5), masked_score)
        weights = jnp.exp(scores - jnp.max(scores, axis=-1, keepdims=True))
        total = jnp.sum(weights, axis=-1, keepdims=True)
        result = jnp.dot(weights.astype(jnp.bfloat16), prompt_values, preferred_element_type=jnp.float32)
        result = (result / total).astype(jnp.bfloat16)
        co_send[i * per : (i + 1) * per] = jnp.concatenate([result, out_pad], axis=1).reshape(per, tok, LANES)
        start_some(co_send, co_recv, co_sems, i * per, per)

    end_exchange(so_send, so_recv, so_sems)
    merged = []
    for n in range(HEADS):
        block = so_recv[n].astype(jnp.float32)
        stale_base = block[:, HD : HD + 1]
        stale_total = block[:, HD + 1 : HD + 2] + block[:, HD + 2 : HD + 3]
        own_base = fresh_stats[n * tok : (n + 1) * tok, 0:1]
        own_total = fresh_stats[n * tok : (n + 1) * tok, 1:2]
        top = jnp.maximum(stale_base, own_base)
        stale_share = stale_total * jnp.exp(stale_base - top)
        own_scale = jnp.exp(own_base - top)
        both = stale_share + own_total * own_scale
        merged.append(
            block[:, :HD] * (stale_share / both) + fresh_blend[:, n * HD : (n + 1) * HD] * (own_scale / both)
        )
    self_out_ref[0] = jnp.concatenate(merged, axis=1)
    for pos in range(inner):

        @pl.when(pos < deep)
        def _():
            outward(pos).wait_send()

    def drain(pos, _):
        for k in range(len(SUM_CUTS)):

            @pl.when((pos > deep) & (deep < inner))
            def _():
                inward(pos, k).wait_send()

            @pl.when((pos > deep) & (deep == inner))
            def _():
                across(pos, k).wait_send()

        return 0

    lax.fori_loop(0, LINE, drain, 0)
    for pos in range(LINE):
        to_twin(pos).wait_send()
    for k in cuts:
        to_half(k).wait_send()
        for i in range(1, n_x):
            x_copy(i, h, k).wait_send()
            x_copy(i, 1 - h, k).wait_send()
        for i in range(1, n_y):
            y_copy(i, k).wait_send()
        for i in range(HALF):
            spread(here, i, i, k).wait_send()
        for i in range(1, HALF):
            spread(there, i, HALF - 1 + i, k).wait_send()

        def drain_twin(g, _):
            to_other_core(c, g, k).wait_send()
            return 0

        lax.fori_loop(0, LINE, drain_twin, 0)
    drain_exchange(cq_send, cq_recv, cq_sems)
    drain_exchange(sf_send, sf_recv, sf_sems)
    drain_exchange(so_send, so_recv, so_sems)
    end_exchange(co_send, co_recv, co_sems)
    cross_out_ref[0] = jnp.concatenate([co_recv[n][:, :HD].astype(jnp.float32) for n in range(HEADS)], axis=1)

    drain_exchange(co_send, co_recv, co_sems)


def shards(
    dims,
    image_queries,
    cross_queries,
    fresh_kv,
    stale_kv,
    prompt_states,
    caption_weight,
    cross_kv_weight,
    prompt_lengths,
    prompt_route,
):
    n_y, n_h, n_x = dims
    operands = (
        prompt_states,
        caption_weight,
        cross_kv_weight.T,
        image_queries,
        cross_queries,
        fresh_kv,
        stale_kv,
    )
    tok, width = image_queries.shape[1:]
    piece = (TILES, TILE, LANES)
    dma = pltpu.SemaphoreType.DMA
    vmem = pl.BlockSpec(memory_space=pltpu.VMEM)
    smem = pl.BlockSpec(memory_space=pltpu.SMEM)
    f32, bf16 = jnp.float32, jnp.bfloat16
    sum_lines, lines, cuts = (LINE, len(SUM_CUTS)), (LINE, len(CUTS)), len(CUTS)
    hbm = pl.BlockSpec(memory_space=pltpu.HBM)
    by_head = pltpu.VMEM((HEADS, tok, LANES), bf16)
    by_head_wide = pltpu.VMEM((HEADS, tok, 2 * LANES), bf16)
    return pl.pallas_call(
        functools.partial(kernel, dims),
        out_shape=[pltpu.VMEM((1, tok, width), f32)] * 2,
        in_specs=[smem, smem] + [hbm] * 7,
        out_specs=[vmem, vmem],
        scratch_shapes=[
            *(pltpu.VMEM(array.shape, bf16) for array in operands),
            pltpu.VMEM((2, LINE, *piece), f32),
            pltpu.VMEM((LINE, *piece), f32),
            pltpu.VMEM((LINE, *piece), f32),
            pltpu.VMEM(piece, f32),
            pltpu.VMEM((HALF, *piece), f32),
            [pltpu.VMEM((n_x, n_h, m, TILE, LANES), bf16) for _, m in CUTS],
            [pltpu.VMEM((n_y, m, TILE, LANES), bf16) for _, m in CUTS],
            [pltpu.VMEM((n_y, m, TILE, LANES), bf16) for _, m in CUTS],
            pltpu.VMEM((2, LINE, *piece), bf16),
            by_head,
            by_head,
            by_head_wide,
            by_head_wide,
            by_head,
            by_head,
            by_head,
            by_head,
            pltpu.VMEM((HEADS * tok, LANES), f32),
            pltpu.VMEM((tok, width), f32),
            dma((len(operands),)),
            dma((2, LINE)),
            dma((2, *sum_lines)),
            dma((2, *sum_lines)),
            dma((2, HALF)),
            dma((2, cuts)),
            dma((2, cuts, n_h, n_x)),
            dma((2, cuts, n_y)),
            dma((LINE - 1, cuts)),
            dma(lines),
            dma((2, *lines)),
            dma((2, HEADS)),
            dma((2, HEADS)),
            dma((2, HEADS)),
            dma((2, HEADS)),
        ],
        compiler_params=pltpu.CompilerParams(
            collective_id=0, has_side_effects=True, vmem_limit_bytes=48 * 1024 * 1024
        ),
    )(prompt_route, prompt_lengths, *(pltpu.with_memory_space_constraint(a, pltpu.HBM) for a in operands))


def solution(mesh, dims=(4, 2, 4)):
    in_specs = (
        P("req", "patch", None),
        P("req", "patch", None),
        P("req", "patch", None),
        P("req", "patch", None),
        P("req", None, "patch"),
        P("patch", None),
        P(None, "patch"),
        P(),
        P(),
    )
    out_specs = (P("req", "patch", None), P("req", "patch", None))
    return jax.shard_map(
        functools.partial(shards, dims), mesh=mesh, in_specs=in_specs, out_specs=out_specs, check_vma=False
    )
```

```python
import functools

import jax
import jax.numpy as jnp
from jax import lax
from jax.experimental import pallas as pl
from jax.experimental.pallas import tpu as pltpu
from jax.sharding import PartitionSpec as P

HEADS = 16
HD = 72
LANES = 128
TILE = 16
TILES = 11
LINE = 8
HALF = LINE // 2
masked_score = -1e30
MESH = pl.DeviceIdType.MESH
SUM_CUTS = ((0, 3), (3, 3), (6, 3), (9, 2))
CUTS = ((0, 6), (6, 5))


def far_first(size):
    return sorted(range(1, size), key=lambda i: -min(i, size - i))


def kernel(
    dims,
    route_ref,
    lengths_ref,
    prompt_hbm,
    caption_w_hbm,
    kv_w_hbm,
    image_q_hbm,
    cross_q_hbm,
    fresh_hbm,
    stale_hbm,
    self_out_ref,
    cross_out_ref,
    prompt_ref,
    caption_w_ref,
    kv_w_ref,
    image_q_ref,
    cross_q_ref,
    fresh_ref,
    stale_ref,
    part,
    sib_part,
    running,
    crossed,
    terms,
    routed,
    y_send,
    y_recv,
    caption,
    cq_send,
    cq_recv,
    sf_send,
    sf_recv,
    so_send,
    so_recv,
    co_send,
    co_recv,
    fresh_stats,
    fresh_blend,
    load_sems,
    sib_sems,
    run_sems,
    cross_sems,
    term_sems,
    h_sems,
    x_sems,
    y_sems,
    gather_send,
    gather_recv,
    twin_sems,
    cq_sems,
    sf_sems,
    so_sems,
    co_sems,
):
    n_y, n_h, n_x = dims
    me_r = lax.axis_index("req")
    me_p = lax.axis_index("patch")
    y = me_r // (n_h * n_x)
    h = (me_r // n_x) % n_h
    x = me_r % n_x
    z = me_p // 2
    c = me_p % 2
    u = z
    shift = h * HALF

    def piece_of(pos):
        return (pos + shift) % LINE

    def patch_peer(i):
        return {"patch": (me_p + i) % (2 * LINE)}

    twin = {"patch": 2 * z + 1 - c}
    half_peer = {"req": me_r + n_x * (1 - 2 * h), "patch": 2 * ((z + HALF) % LINE) + c}

    def x_peer(i):
        return {"req": me_r - x + (x + i) % n_x}

    def y_peer(i):
        return {"req": ((y + i) % n_y) * (n_h * n_x) + h * n_x + x}

    def copy(src, dst, send, recv, device):
        return pltpu.make_async_remote_copy(
            src_ref=src, dst_ref=dst, send_sem=send, recv_sem=recv, device_id=device, device_id_type=MESH
        )

    loads = [
        pltpu.make_async_copy(src, dst, load_sems.at[i])
        for i, (src, dst) in enumerate(
            (
                (prompt_hbm, prompt_ref),
                (caption_w_hbm, caption_w_ref),
                (cross_q_hbm, cross_q_ref),
                (image_q_hbm, image_q_ref),
                (stale_hbm, stale_ref),
                (fresh_hbm, fresh_ref),
                (kv_w_hbm, kv_w_ref),
            )
        )
    ]
    barrier = pltpu.get_barrier_semaphore()
    greeted = 0
    for device in (
        [patch_peer(i) for i in range(1, 2 * LINE)]
        + [half_peer]
        + [x_peer(i) for i in range(1, n_x)]
        + [y_peer(i) for i in range(1, n_y)]
    ):
        pl.semaphore_signal(barrier, inc=1, device_id=device, device_id_type=MESH)
        greeted += 1
    for load in loads:
        load.start()

    loads[0].wait()
    loads[1].wait()
    prompt = prompt_ref[0]
    rows = prompt.shape[0]
    row_tiles = -(-rows // TILE)
    prompt = jnp.concatenate(
        [prompt, jnp.zeros((row_tiles * TILE - rows, prompt.shape[1]), prompt.dtype)], axis=0
    )
    width = caption_w_ref.shape[1]
    col_tiles = width // LANES

    def place(i, j):
        piece, at = divmod(i * col_tiles + j, TILES)
        return piece // LINE, piece % LINE, at

    slots = [piece_of(g) for g in range(LINE)]

    group = 3
    for j0 in range(0, col_tiles, group):
        block = jnp.dot(
            prompt, caption_w_ref[:, j0 * LANES : (j0 + group) * LANES], preferred_element_type=jnp.float32
        )
        for i in range(row_tiles):
            for j in range(group):
                core, g, at = place(i, j0 + j)
                part[core, slots[g], at] = block[i * TILE : (i + 1) * TILE, j * LANES : (j + 1) * LANES]
    for t in range(row_tiles * col_tiles, 2 * LINE * TILES):
        part[t // (LINE * TILES), slots[(t // TILES) % LINE], t % TILES] = jnp.zeros((TILE, LANES), jnp.float32)

    left = u < HALF
    deep = jnp.where(left, u, LINE - 1 - u)

    def at(pos):
        return jnp.where(left, pos, LINE - 1 - pos)

    def to_twin(pos):
        return copy(part.at[1 - c, at(pos)], sib_part.at[at(pos)], sib_sems.at[0, pos], sib_sems.at[1, pos], twin)

    pl.semaphore_wait(barrier, greeted)
    for pos in reversed(range(LINE)):
        to_twin(pos).start()
    for load in loads[2:]:
        load.wait()

    tok = image_q_ref.shape[1]
    pad_c = jnp.zeros((tok, LANES - HD), jnp.bfloat16)
    pad_s = jnp.zeros((tok, 2 * LANES - 3 * HD), jnp.bfloat16)
    for n in range(HEADS):
        a, b = n * HD, (n + 1) * HD
        cq_send[n] = jnp.concatenate([cross_q_ref[0, :, a:b], pad_c], axis=1)
        sf_send[n] = jnp.concatenate(
            [
                image_q_ref[0, :, a:b],
                stale_ref[0, :, a:b],
                stale_ref[0, :, width + a : width + b],
                pad_s,
            ],
            axis=1,
        )

    def exchange(send, recv, sems, i):
        peer = (me_p + i) % (2 * LINE)
        return copy(send.at[peer], recv.at[me_p], sems.at[0, i], sems.at[1, i], {"patch": peer})

    def arrival(send, recv, sems, i):
        origin = (me_p - i + 2 * LINE) % (2 * LINE)
        return copy(send.at[origin], recv.at[origin], sems.at[0, i], sems.at[1, i], {"patch": origin})

    def start_exchange(send, recv, sems):
        recv[me_p] = send[me_p]

        def step(i, _):
            exchange(send, recv, sems, i).start()
            return 0

        lax.fori_loop(1, 2 * LINE, step, 0)

    def start_some(send, recv, sems, first, count):
        def step(n, _):
            @pl.when(n == me_p)
            def _():
                recv[n] = send[n]

            @pl.when(n != me_p)
            def _():
                exchange(send, recv, sems, (n - me_p + 2 * LINE) % (2 * LINE)).start()

            return 0

        lax.fori_loop(first, first + count, step, 0)

    def end_exchange(send, recv, sems):
        def step(i, _):
            arrival(send, recv, sems, i).wait_recv()
            return 0

        lax.fori_loop(1, 2 * LINE, step, 0)

    def drain_exchange(send, recv, sems):
        def step(i, _):
            exchange(send, recv, sems, i).wait_send()
            return 0

        lax.fori_loop(1, 2 * LINE, step, 0)

    start_exchange(cq_send, cq_recv, cq_sems)
    sums = part.at[c]

    def add_twin(pos):
        to_twin(pos).wait_recv()
        sums[at(pos)] = sums[at(pos)] + sib_part[at(pos)]

    inner = HALF - 1
    def at_device(pos):
        return {"patch": 2 * at(pos) + c}

    def sum_cut(k):
        a, m = SUM_CUTS[k]
        return pl.ds(a, m)

    def inward(pos, k):
        return copy(
            sums.at[at(pos), sum_cut(k)],
            running.at[at(pos), sum_cut(k)],
            run_sems.at[0, pos, k],
            run_sems.at[1, pos, k],
            at_device(jnp.minimum(deep + 1, inner)),
        )

    def across(pos, k):
        return copy(
            sums.at[at(pos), sum_cut(k)],
            crossed.at[sum_cut(k)],
            cross_sems.at[0, pos, k],
            cross_sems.at[1, 0, k],
            at_device(pos),
        )

    def outward(pos):
        return copy(
            sums.at[at(pos)], terms.at[deep], term_sems.at[0, pos], term_sems.at[1, deep], at_device(pos)
        )

    def term_arrival(pos):
        return copy(sums.at[u], terms.at[pos], term_sems.at[0, 0], term_sems.at[1, pos], at_device(pos))

    def first_step(t, _):
        pos = LINE - 1 - t
        add_twin(pos)

        @pl.when(pos < deep)
        def _():
            outward(pos).start()

        return 0

    @pl.when(deep > 0)
    def _():
        lax.fori_loop(0, LINE, first_step, 0)

    def reduce_step(t, _):
        pos = LINE - 1 - t

        @pl.when(deep == 0)
        def _():
            add_twin(pos)

        @pl.when(pos >= deep)
        def _():
            for k in range(len(SUM_CUTS)):

                @pl.when(deep > 0)
                def _():
                    inward(pos, k).wait_recv()
                    sums[at(pos), sum_cut(k)] = sums[at(pos), sum_cut(k)] + running[at(pos), sum_cut(k)]

                @pl.when((pos > deep) & (deep < inner))
                def _():
                    inward(pos, k).start()

                @pl.when((pos > deep) & (deep == inner))
                def _():
                    across(pos, k).start()

        return 0

    lax.fori_loop(0, LINE, reduce_step, 0)
    for pos in range(1, HALF):

        @pl.when(pos > deep)
        def _():
            term_arrival(pos).wait_recv()
            sums[u] = sums[u] + terms[pos]

    for k in range(len(SUM_CUTS)):
        across(inner + 1, k).wait_recv()

    def to_half(k):
        ref = routed[k].at[x, h]
        return copy(ref, ref, h_sems.at[0, k], h_sems.at[1, k], half_peer)

    def half_arrival(k):
        ref = routed[k].at[x, 1 - h]
        return copy(ref, ref, h_sems.at[0, k], h_sems.at[1, k], half_peer)

    def x_copy(i, half, k):
        ref = routed[k].at[x, half]
        return copy(ref, ref, x_sems.at[0, k, half, i], x_sems.at[1, k, half, i], x_peer(i))

    def x_arrival(i, half, k):
        ref = routed[k].at[(x - i + n_x) % n_x, half]
        return copy(ref, ref, x_sems.at[0, k, half, i], x_sems.at[1, k, half, i], x_peer(i))

    def wanted(i, k):
        source = route_ref[((y + i) % n_y) * (n_h * n_x) + h * n_x + x]
        return routed[k][lax.rem(source, n_x), lax.rem(lax.div(source, n_x), n_h)]

    def y_copy(i, k):
        return copy(y_send[k].at[i], y_recv[k].at[y], y_sems.at[0, k, i], y_sems.at[1, k, i], y_peer(i))

    def y_arrival(i, k):
        ref = y_recv[k].at[(y - i + n_y) % n_y]
        return copy(ref, ref, y_sems.at[0, k, i], y_sems.at[1, k, i], y_peer(i))

    here = piece_of(u)
    there = piece_of((u + HALF) % LINE)

    def beside(i):
        return (u // HALF) * HALF + (u + i) % HALF

    def tiles_of(core, g, k):
        a, m = CUTS[k]
        return caption.at[core, g, pl.ds(a, m)]

    def spread(g, i, n, k):
        pos = beside(i) if i else (u + HALF) % LINE
        ref = tiles_of(c, g, k)
        return copy(ref, ref, gather_send.at[n, k], gather_recv.at[g, k], {"patch": 2 * pos + c})

    def gathered(g, k):
        ref = tiles_of(c, g, k)
        return copy(ref, ref, gather_send.at[0, k], gather_recv.at[g, k], twin)

    def to_other_core(core, g, k):
        ref = tiles_of(core, g, k)
        return copy(ref, ref, twin_sems.at[0, g, k], twin_sems.at[1, g, k], twin)

    cuts = range(len(CUTS))
    for k, (a, m) in enumerate(CUTS):
        piece = sums[u, a : a + m] + crossed[a : a + m]
        piece = jax.nn.gelu(piece, approximate=True).astype(jnp.bfloat16)
        routed[k][x, h] = piece
        to_half(k).start()
        for i in far_first(n_x):
            x_copy(i, h, k).start()
    seq = 2 * LINE * tok
    contract_last = (((1,), (1,)), ((), ()))
    chunk = LANES
    per = chunk // tok
    zero = jnp.zeros((), jnp.bfloat16)
    head_of = lax.broadcasted_iota(jnp.int32, (tok, width), 1) // HD

    def apart(rows):
        return jnp.concatenate([jnp.where(head_of == n, rows, zero) for n in range(HEADS)], axis=0)

    fresh_scores = lax.dot_general(
        apart(image_q_ref[0]), fresh_ref[0, :, :width], contract_last, preferred_element_type=jnp.float32
    )
    fresh_scores = fresh_scores * HD ** (-0.5)
    fresh_base = jnp.max(fresh_scores, axis=-1, keepdims=True)
    fresh_weights = jnp.exp(fresh_scores - fresh_base)
    fresh_total = jnp.sum(fresh_weights, axis=-1, keepdims=True)
    fresh_weights = fresh_weights.astype(jnp.bfloat16)
    fresh_stats[:, 0:1] = fresh_base
    fresh_stats[:, 1:2] = fresh_total
    fresh_blend[...] = jnp.dot(
        jnp.concatenate([fresh_weights[n * tok : (n + 1) * tok] for n in range(HEADS)], axis=1),
        apart(fresh_ref[0, :, width:]),
        preferred_element_type=jnp.float32,
    )

    for k in cuts:
        half_arrival(k).wait_recv()
        for i in far_first(n_x):
            x_copy(i, 1 - h, k).start()
    start_exchange(sf_send, sf_recv, sf_sems)
    for k in cuts:
        for i in range(1, n_x):
            x_arrival(i, h, k).wait_recv()
            x_arrival(i, 1 - h, k).wait_recv()
        for i in far_first(n_y):
            y_send[k][i] = wanted(i, k)
            y_copy(i, k).start()
        y_recv[k][y] = wanted(0, k)
    source = route_ref[me_r]
    for k, (a, m) in enumerate(CUTS):
        for i in range(1, n_y):
            y_arrival(i, k).wait_recv()
        caption[c, here, a : a + m] = y_recv[k][lax.div(source, n_h * n_x)]
        spread(here, 0, 0, k).start()
    for k in cuts:
        for i in range(1, HALF):
            spread(here, i, i, k).start()
        to_other_core(c, here, k).start()

    for k in cuts:
        gathered(there, k).wait_recv()
        for i in range(1, HALF):
            spread(there, i, HALF - 1 + i, k).start()
        to_other_core(c, there, k).start()
    end_exchange(sf_send, sf_recv, sf_sems)
    whole = sf_recv[...].reshape(seq, 2 * LANES)
    queries, keys, values = whole[:, :HD], whole[:, HD : 2 * HD], whole[:, 2 * HD : 3 * HD]
    own = (
        lax.broadcasted_iota(jnp.int32, (chunk, chunk), 0) // tok
        == lax.broadcasted_iota(jnp.int32, (chunk, chunk), 1) // tok
    )
    self_pad = jnp.zeros((chunk, LANES - HD - 3), jnp.bfloat16)
    for i in range(seq // chunk):
        a, b = i * chunk, (i + 1) * chunk
        scores = lax.dot_general(queries[a:b], keys, contract_last, preferred_element_type=jnp.float32)
        scores = scores * HD ** (-0.5)
        mixed = [jnp.where(own, masked_score, scores[:, a:b])]
        if a > 0:
            mixed = [scores[:, :a]] + mixed
        if b < seq:
            mixed = mixed + [scores[:, b:]]
        scores = jnp.concatenate(mixed, axis=1)
        base = jnp.max(scores, axis=-1, keepdims=True).astype(jnp.bfloat16)
        weights = jnp.exp(scores - base.astype(jnp.float32))
        total = jnp.sum(weights, axis=-1, keepdims=True)
        result = jnp.dot(weights.astype(jnp.bfloat16), values, preferred_element_type=jnp.float32)
        result = (result / total).astype(jnp.bfloat16)
        total_high = total.astype(jnp.bfloat16)
        total_low = (total - total_high.astype(jnp.float32)).astype(jnp.bfloat16)
        so_send[i * per : (i + 1) * per] = jnp.concatenate(
            [result, base, total_high, total_low, self_pad], axis=1
        ).reshape(per, tok, LANES)
        start_some(so_send, so_recv, so_sems, i * per, per)

    for far in (0, HALF):
        for k in cuts:
            for i in range(1, HALF):
                g = piece_of((beside(i) + far) % LINE)
                gathered(g, k).wait_recv()
                to_other_core(c, g, k).start()

    end_exchange(cq_send, cq_recv, cq_sems)

    def twin_wait(q, _):
        for k in range(len(CUTS)):
            to_other_core(1 - c, q, k).wait_recv()
        return 0

    lax.fori_loop(0, LINE, twin_wait, 0)
    caption_rows = jnp.concatenate(
        [jnp.concatenate([caption[place(i, j)] for j in range(col_tiles)], axis=1) for i in range(row_tiles)], axis=0
    )
    head_states = lax.dot_general(
        caption_rows, kv_w_ref[...], contract_last, preferred_element_type=jnp.float32
    ).astype(jnp.bfloat16)
    prompt_keys, prompt_values = head_states[:, :HD], head_states[:, HD : 2 * HD]
    out_pad = jnp.zeros((chunk, LANES - HD), jnp.bfloat16)
    length = lengths_ref[source]
    visible = lax.broadcasted_iota(jnp.int32, (1, row_tiles * TILE), 1) < length
    cross_rows = cq_recv[...].reshape(seq, LANES)[:, :HD]
    for i in range(seq // chunk):
        a, b = i * chunk, (i + 1) * chunk
        scores = lax.dot_general(cross_rows[a:b], prompt_keys, contract_last, preferred_element_type=jnp.float32)
        scores = jnp.where(visible, scores * HD ** (-0.5), masked_score)
        weights = jnp.exp(scores - jnp.max(scores, axis=-1, keepdims=True))
        total = jnp.sum(weights, axis=-1, keepdims=True)
        result = jnp.dot(weights.astype(jnp.bfloat16), prompt_values, preferred_element_type=jnp.float32)
        result = (result / total).astype(jnp.bfloat16)
        co_send[i * per : (i + 1) * per] = jnp.concatenate([result, out_pad], axis=1).reshape(per, tok, LANES)
        start_some(co_send, co_recv, co_sems, i * per, per)

    end_exchange(so_send, so_recv, so_sems)
    merged = []
    for n in range(HEADS):
        block = so_recv[n].astype(jnp.float32)
        stale_base = block[:, HD : HD + 1]
        stale_total = block[:, HD + 1 : HD + 2] + block[:, HD + 2 : HD + 3]
        own_base = fresh_stats[n * tok : (n + 1) * tok, 0:1]
        own_total = fresh_stats[n * tok : (n + 1) * tok, 1:2]
        top = jnp.maximum(stale_base, own_base)
        stale_share = stale_total * jnp.exp(stale_base - top)
        own_scale = jnp.exp(own_base - top)
        both = stale_share + own_total * own_scale
        merged.append(
            block[:, :HD] * (stale_share / both) + fresh_blend[:, n * HD : (n + 1) * HD] * (own_scale / both)
        )
    self_out_ref[0] = jnp.concatenate(merged, axis=1)
    for pos in range(inner):

        @pl.when(pos < deep)
        def _():
            outward(pos).wait_send()

    def drain(pos, _):
        for k in range(len(SUM_CUTS)):

            @pl.when((pos > deep) & (deep < inner))
            def _():
                inward(pos, k).wait_send()

            @pl.when((pos > deep) & (deep == inner))
            def _():
                across(pos, k).wait_send()

        return 0

    lax.fori_loop(0, LINE, drain, 0)
    for pos in range(LINE):
        to_twin(pos).wait_send()
    for k in cuts:
        to_half(k).wait_send()
        for i in range(1, n_x):
            x_copy(i, h, k).wait_send()
            x_copy(i, 1 - h, k).wait_send()
        for i in range(1, n_y):
            y_copy(i, k).wait_send()
        for i in range(HALF):
            spread(here, i, i, k).wait_send()
        for i in range(1, HALF):
            spread(there, i, HALF - 1 + i, k).wait_send()

        def drain_twin(g, _):
            to_other_core(c, g, k).wait_send()
            return 0

        lax.fori_loop(0, LINE, drain_twin, 0)
    drain_exchange(cq_send, cq_recv, cq_sems)
    drain_exchange(sf_send, sf_recv, sf_sems)
    drain_exchange(so_send, so_recv, so_sems)
    end_exchange(co_send, co_recv, co_sems)
    cross_out_ref[0] = jnp.concatenate([co_recv[n][:, :HD].astype(jnp.float32) for n in range(HEADS)], axis=1)

    drain_exchange(co_send, co_recv, co_sems)


def shards(
    dims,
    image_queries,
    cross_queries,
    fresh_kv,
    stale_kv,
    prompt_states,
    caption_weight,
    cross_kv_weight,
    prompt_lengths,
    prompt_route,
):
    n_y, n_h, n_x = dims
    operands = (
        prompt_states,
        caption_weight,
        cross_kv_weight.T,
        image_queries,
        cross_queries,
        fresh_kv,
        stale_kv,
    )
    tok, width = image_queries.shape[1:]
    piece = (TILES, TILE, LANES)
    dma = pltpu.SemaphoreType.DMA
    vmem = pl.BlockSpec(memory_space=pltpu.VMEM)
    smem = pl.BlockSpec(memory_space=pltpu.SMEM)
    f32, bf16 = jnp.float32, jnp.bfloat16
    sum_lines, lines, cuts = (LINE, len(SUM_CUTS)), (LINE, len(CUTS)), len(CUTS)
    hbm = pl.BlockSpec(memory_space=pltpu.HBM)
    by_head = pltpu.VMEM((HEADS, tok, LANES), bf16)
    by_head_wide = pltpu.VMEM((HEADS, tok, 2 * LANES), bf16)
    return pl.pallas_call(
        functools.partial(kernel, dims),
        out_shape=[pltpu.VMEM((1, tok, width), f32)] * 2,
        in_specs=[smem, smem] + [hbm] * 7,
        out_specs=[vmem, vmem],
        scratch_shapes=[
            *(pltpu.VMEM(array.shape, bf16) for array in operands),
            pltpu.VMEM((2, LINE, *piece), f32),
            pltpu.VMEM((LINE, *piece), f32),
            pltpu.VMEM((LINE, *piece), f32),
            pltpu.VMEM(piece, f32),
            pltpu.VMEM((HALF, *piece), f32),
            [pltpu.VMEM((n_x, n_h, m, TILE, LANES), bf16) for _, m in CUTS],
            [pltpu.VMEM((n_y, m, TILE, LANES), bf16) for _, m in CUTS],
            [pltpu.VMEM((n_y, m, TILE, LANES), bf16) for _, m in CUTS],
            pltpu.VMEM((2, LINE, *piece), bf16),
            by_head,
            by_head,
            by_head_wide,
            by_head_wide,
            by_head,
            by_head,
            by_head,
            by_head,
            pltpu.VMEM((HEADS * tok, LANES), f32),
            pltpu.VMEM((tok, width), f32),
            dma((len(operands),)),
            dma((2, LINE)),
            dma((2, *sum_lines)),
            dma((2, *sum_lines)),
            dma((2, HALF)),
            dma((2, cuts)),
            dma((2, cuts, n_h, n_x)),
            dma((2, cuts, n_y)),
            dma((LINE - 1, cuts)),
            dma(lines),
            dma((2, *lines)),
            dma((2, HEADS)),
            dma((2, HEADS)),
            dma((2, HEADS)),
            dma((2, HEADS)),
        ],
        compiler_params=pltpu.CompilerParams(
            collective_id=0, has_side_effects=True, vmem_limit_bytes=48 * 1024 * 1024
        ),
    )(prompt_route, prompt_lengths, *(pltpu.with_memory_space_constraint(a, pltpu.HBM) for a in operands))


def solution(mesh, dims=(4, 2, 4)):
    in_specs = (
        P("req", "patch", None),
        P("req", "patch", None),
        P("req", "patch", None),
        P("req", "patch", None),
        P("req", None, "patch"),
        P("patch", None),
        P(None, "patch"),
        P(),
        P(),
    )
    out_specs = (P("req", "patch", None), P("req", "patch", None))
    return jax.shard_map(
        functools.partial(shards, dims), mesh=mesh, in_specs=in_specs, out_specs=out_specs, check_vma=False
    )
```

```python
import functools

import jax
import jax.numpy as jnp
from jax import lax
from jax.experimental import pallas as pl
from jax.experimental.pallas import tpu as pltpu
from jax.sharding import PartitionSpec as P

HEADS = 16
HD = 72
LANES = 128
TILE = 16
TILES = 11
LINE = 8
HALF = LINE // 2
masked_score = -1e30
MESH = pl.DeviceIdType.MESH
SUM_CUTS = ((0, 3), (3, 3), (6, 3), (9, 2))
CUTS = ((0, 6), (6, 5))


def far_first(size):
    return sorted(range(1, size), key=lambda i: -min(i, size - i))


def kernel(
    dims,
    route_ref,
    lengths_ref,
    prompt_hbm,
    caption_w_hbm,
    kv_w_hbm,
    image_q_hbm,
    cross_q_hbm,
    fresh_hbm,
    stale_hbm,
    out_ref,
    prompt_ref,
    caption_w_ref,
    kv_w_ref,
    image_q_ref,
    cross_q_ref,
    fresh_ref,
    stale_ref,
    part,
    sib_part,
    running,
    crossed,
    terms,
    routed,
    y_send,
    y_recv,
    caption,
    cq_send,
    cq_recv,
    sf_send,
    sf_recv,
    so_send,
    so_recv,
    co_send,
    co_recv,
    fresh_stats,
    fresh_blend,
    load_sems,
    sib_sems,
    run_sems,
    cross_sems,
    term_sems,
    h_sems,
    x_sems,
    y_sems,
    gather_send,
    gather_recv,
    twin_sems,
    cq_sems,
    sf_sems,
    so_sems,
    co_sems,
):
    n_y, n_h, n_x = dims
    me_r = lax.axis_index("req")
    me_p = lax.axis_index("patch")
    y = me_r // (n_h * n_x)
    h = (me_r // n_x) % n_h
    x = me_r % n_x
    z = me_p // 2
    c = me_p % 2
    u = z
    shift = h * HALF

    def piece_of(pos):
        return (pos + shift) % LINE

    def patch_peer(i):
        return {"patch": (me_p + i) % (2 * LINE)}

    twin = {"patch": 2 * z + 1 - c}
    half_peer = {"req": me_r + n_x * (1 - 2 * h), "patch": 2 * ((z + HALF) % LINE) + c}

    def x_peer(i):
        return {"req": me_r - x + (x + i) % n_x}

    def y_peer(i):
        return {"req": ((y + i) % n_y) * (n_h * n_x) + h * n_x + x}

    def copy(src, dst, send, recv, device):
        return pltpu.make_async_remote_copy(
            src_ref=src, dst_ref=dst, send_sem=send, recv_sem=recv, device_id=device, device_id_type=MESH
        )

    loads = [
        pltpu.make_async_copy(src, dst, load_sems.at[i])
        for i, (src, dst) in enumerate(
            (
                (prompt_hbm, prompt_ref),
                (caption_w_hbm, caption_w_ref),
                (cross_q_hbm, cross_q_ref),
                (image_q_hbm, image_q_ref),
                (stale_hbm, stale_ref),
                (fresh_hbm, fresh_ref),
                (kv_w_hbm, kv_w_ref),
            )
        )
    ]
    barrier = pltpu.get_barrier_semaphore()
    greeted = 0
    for device in (
        [patch_peer(i) for i in range(1, 2 * LINE)]
        + [half_peer]
        + [x_peer(i) for i in range(1, n_x)]
        + [y_peer(i) for i in range(1, n_y)]
    ):
        pl.semaphore_signal(barrier, inc=1, device_id=device, device_id_type=MESH)
        greeted += 1
    for load in loads:
        load.start()

    loads[0].wait()
    loads[1].wait()
    prompt = prompt_ref[0]
    rows = prompt.shape[0]
    row_tiles = -(-rows // TILE)
    prompt = jnp.concatenate(
        [prompt, jnp.zeros((row_tiles * TILE - rows, prompt.shape[1]), prompt.dtype)], axis=0
    )
    width = caption_w_ref.shape[1]
    col_tiles = width // LANES

    def place(i, j):
        piece, at = divmod(i * col_tiles + j, TILES)
        return piece // LINE, piece % LINE, at

    slots = [piece_of(g) for g in range(LINE)]

    group = 3
    for j0 in range(0, col_tiles, group):
        block = jnp.dot(
            prompt, caption_w_ref[:, j0 * LANES : (j0 + group) * LANES], preferred_element_type=jnp.float32
        )
        for i in range(row_tiles):
            for j in range(group):
                core, g, at = place(i, j0 + j)
                part[core, slots[g], at] = block[i * TILE : (i + 1) * TILE, j * LANES : (j + 1) * LANES]
    for t in range(row_tiles * col_tiles, 2 * LINE * TILES):
        part[t // (LINE * TILES), slots[(t // TILES) % LINE], t % TILES] = jnp.zeros((TILE, LANES), jnp.float32)

    left = u < HALF
    deep = jnp.where(left, u, LINE - 1 - u)

    def at(pos):
        return jnp.where(left, pos, LINE - 1 - pos)

    def to_twin(pos):
        return copy(part.at[1 - c, at(pos)], sib_part.at[at(pos)], sib_sems.at[0, pos], sib_sems.at[1, pos], twin)

    pl.semaphore_wait(barrier, greeted)
    for pos in reversed(range(LINE)):
        to_twin(pos).start()
    for load in loads[2:]:
        load.wait()

    tok = image_q_ref.shape[1]
    pad_c = jnp.zeros((tok, LANES - HD), jnp.bfloat16)
    pad_s = jnp.zeros((tok, 2 * LANES - 3 * HD), jnp.bfloat16)
    for n in range(HEADS):
        a, b = n * HD, (n + 1) * HD
        cq_send[n] = jnp.concatenate([cross_q_ref[0, :, a:b], pad_c], axis=1)
        sf_send[n] = jnp.concatenate(
            [
                image_q_ref[0, :, a:b],
                stale_ref[0, :, a:b],
                stale_ref[0, :, width + a : width + b],
                pad_s,
            ],
            axis=1,
        )

    def exchange(send, recv, sems, i):
        peer = (me_p + i) % (2 * LINE)
        return copy(send.at[peer], recv.at[me_p], sems.at[0, i], sems.at[1, i], {"patch": peer})

    def arrival(send, recv, sems, i):
        origin = (me_p - i + 2 * LINE) % (2 * LINE)
        return copy(send.at[origin], recv.at[origin], sems.at[0, i], sems.at[1, i], {"patch": origin})

    def start_exchange(send, recv, sems):
        recv[me_p] = send[me_p]

        def step(i, _):
            exchange(send, recv, sems, i).start()
            return 0

        lax.fori_loop(1, 2 * LINE, step, 0)

    def start_some(send, recv, sems, first, count):
        def step(n, _):
            @pl.when(n == me_p)
            def _():
                recv[n] = send[n]

            @pl.when(n != me_p)
            def _():
                exchange(send, recv, sems, (n - me_p + 2 * LINE) % (2 * LINE)).start()

            return 0

        lax.fori_loop(first, first + count, step, 0)

    def end_exchange(send, recv, sems):
        def step(i, _):
            arrival(send, recv, sems, i).wait_recv()
            return 0

        lax.fori_loop(1, 2 * LINE, step, 0)

    def drain_exchange(send, recv, sems):
        def step(i, _):
            exchange(send, recv, sems, i).wait_send()
            return 0

        lax.fori_loop(1, 2 * LINE, step, 0)

    start_exchange(cq_send, cq_recv, cq_sems)
    sums = part.at[c]

    def add_twin(pos):
        to_twin(pos).wait_recv()
        sums[at(pos)] = sums[at(pos)] + sib_part[at(pos)]

    inner = HALF - 1
    def at_device(pos):
        return {"patch": 2 * at(pos) + c}

    def sum_cut(k):
        a, m = SUM_CUTS[k]
        return pl.ds(a, m)

    def inward(pos, k):
        return copy(
            sums.at[at(pos), sum_cut(k)],
            running.at[at(pos), sum_cut(k)],
            run_sems.at[0, pos, k],
            run_sems.at[1, pos, k],
            at_device(jnp.minimum(deep + 1, inner)),
        )

    def across(pos, k):
        return copy(
            sums.at[at(pos), sum_cut(k)],
            crossed.at[sum_cut(k)],
            cross_sems.at[0, pos, k],
            cross_sems.at[1, 0, k],
            at_device(pos),
        )

    def outward(pos):
        return copy(
            sums.at[at(pos)], terms.at[deep], term_sems.at[0, pos], term_sems.at[1, deep], at_device(pos)
        )

    def term_arrival(pos):
        return copy(sums.at[u], terms.at[pos], term_sems.at[0, 0], term_sems.at[1, pos], at_device(pos))

    def first_step(t, _):
        pos = LINE - 1 - t
        add_twin(pos)

        @pl.when(pos < deep)
        def _():
            outward(pos).start()

        return 0

    @pl.when(deep > 0)
    def _():
        lax.fori_loop(0, LINE, first_step, 0)

    def reduce_step(t, _):
        pos = LINE - 1 - t

        @pl.when(deep == 0)
        def _():
            add_twin(pos)

        @pl.when(pos >= deep)
        def _():
            for k in range(len(SUM_CUTS)):

                @pl.when(deep > 0)
                def _():
                    inward(pos, k).wait_recv()
                    sums[at(pos), sum_cut(k)] = sums[at(pos), sum_cut(k)] + running[at(pos), sum_cut(k)]

                @pl.when((pos > deep) & (deep < inner))
                def _():
                    inward(pos, k).start()

                @pl.when((pos > deep) & (deep == inner))
                def _():
                    across(pos, k).start()

        return 0

    lax.fori_loop(0, LINE, reduce_step, 0)
    for pos in range(1, HALF):

        @pl.when(pos > deep)
        def _():
            term_arrival(pos).wait_recv()
            sums[u] = sums[u] + terms[pos]

    for k in range(len(SUM_CUTS)):
        across(inner + 1, k).wait_recv()

    def to_half(k):
        ref = routed[k].at[x, h]
        return copy(ref, ref, h_sems.at[0, k], h_sems.at[1, k], half_peer)

    def half_arrival(k):
        ref = routed[k].at[x, 1 - h]
        return copy(ref, ref, h_sems.at[0, k], h_sems.at[1, k], half_peer)

    def x_copy(i, half, k):
        ref = routed[k].at[x, half]
        return copy(ref, ref, x_sems.at[0, k, half, i], x_sems.at[1, k, half, i], x_peer(i))

    def x_arrival(i, half, k):
        ref = routed[k].at[(x - i + n_x) % n_x, half]
        return copy(ref, ref, x_sems.at[0, k, half, i], x_sems.at[1, k, half, i], x_peer(i))

    def wanted(i, k):
        source = route_ref[((y + i) % n_y) * (n_h * n_x) + h * n_x + x]
        return routed[k][lax.rem(source, n_x), lax.rem(lax.div(source, n_x), n_h)]

    def y_copy(i, k):
        return copy(y_send[k].at[i], y_recv[k].at[y], y_sems.at[0, k, i], y_sems.at[1, k, i], y_peer(i))

    def y_arrival(i, k):
        ref = y_recv[k].at[(y - i + n_y) % n_y]
        return copy(ref, ref, y_sems.at[0, k, i], y_sems.at[1, k, i], y_peer(i))

    here = piece_of(u)
    there = piece_of((u + HALF) % LINE)

    def beside(i):
        return (u // HALF) * HALF + (u + i) % HALF

    def tiles_of(core, g, k):
        a, m = CUTS[k]
        return caption.at[core, g, pl.ds(a, m)]

    def spread(g, i, n, k):
        pos = beside(i) if i else (u + HALF) % LINE
        ref = tiles_of(c, g, k)
        return copy(ref, ref, gather_send.at[n, k], gather_recv.at[g, k], {"patch": 2 * pos + c})

    def gathered(g, k):
        ref = tiles_of(c, g, k)
        return copy(ref, ref, gather_send.at[0, k], gather_recv.at[g, k], twin)

    def to_other_core(core, g, k):
        ref = tiles_of(core, g, k)
        return copy(ref, ref, twin_sems.at[0, g, k], twin_sems.at[1, g, k], twin)

    cuts = range(len(CUTS))
    for k, (a, m) in enumerate(CUTS):
        piece = sums[u, a : a + m] + crossed[a : a + m]
        piece = jax.nn.gelu(piece, approximate=True).astype(jnp.bfloat16)
        routed[k][x, h] = piece
        to_half(k).start()
        for i in far_first(n_x):
            x_copy(i, h, k).start()
    seq = 2 * LINE * tok
    contract_last = (((1,), (1,)), ((), ()))
    chunk = LANES
    per = chunk // tok
    zero = jnp.zeros((), jnp.bfloat16)
    head_of = lax.broadcasted_iota(jnp.int32, (tok, width), 1) // HD

    def apart(rows):
        return jnp.concatenate([jnp.where(head_of == n, rows, zero) for n in range(HEADS)], axis=0)

    fresh_scores = lax.dot_general(
        apart(image_q_ref[0]), fresh_ref[0, :, :width], contract_last, preferred_element_type=jnp.float32
    )
    fresh_scores = fresh_scores * HD ** (-0.5)
    fresh_base = jnp.max(fresh_scores, axis=-1, keepdims=True)
    fresh_weights = jnp.exp(fresh_scores - fresh_base)
    fresh_total = jnp.sum(fresh_weights, axis=-1, keepdims=True)
    fresh_weights = fresh_weights.astype(jnp.bfloat16)
    fresh_stats[:, 0:1] = fresh_base
    fresh_stats[:, 1:2] = fresh_total
    fresh_blend[...] = jnp.dot(
        jnp.concatenate([fresh_weights[n * tok : (n + 1) * tok] for n in range(HEADS)], axis=1),
        apart(fresh_ref[0, :, width:]),
        preferred_element_type=jnp.float32,
    )

    for k in cuts:
        half_arrival(k).wait_recv()
        for i in far_first(n_x):
            x_copy(i, 1 - h, k).start()
    start_exchange(sf_send, sf_recv, sf_sems)
    for k in cuts:
        for i in range(1, n_x):
            x_arrival(i, h, k).wait_recv()
            x_arrival(i, 1 - h, k).wait_recv()
        for i in far_first(n_y):
            y_send[k][i] = wanted(i, k)
            y_copy(i, k).start()
        y_recv[k][y] = wanted(0, k)
    source = route_ref[me_r]
    for k, (a, m) in enumerate(CUTS):
        for i in range(1, n_y):
            y_arrival(i, k).wait_recv()
        caption[c, here, a : a + m] = y_recv[k][lax.div(source, n_h * n_x)]
        spread(here, 0, 0, k).start()
    for k in cuts:
        for i in range(1, HALF):
            spread(here, i, i, k).start()
        to_other_core(c, here, k).start()

    for k in cuts:
        gathered(there, k).wait_recv()
        for i in range(1, HALF):
            spread(there, i, HALF - 1 + i, k).start()
        to_other_core(c, there, k).start()
    end_exchange(sf_send, sf_recv, sf_sems)
    whole = sf_recv[...].reshape(seq, 2 * LANES)
    queries, keys, values = whole[:, :HD], whole[:, HD : 2 * HD], whole[:, 2 * HD : 3 * HD]
    own = (
        lax.broadcasted_iota(jnp.int32, (chunk, chunk), 0) // tok
        == lax.broadcasted_iota(jnp.int32, (chunk, chunk), 1) // tok
    )
    self_pad = jnp.zeros((chunk, LANES - HD - 3), jnp.bfloat16)
    for i in range(seq // chunk):
        a, b = i * chunk, (i + 1) * chunk
        scores = lax.dot_general(queries[a:b], keys, contract_last, preferred_element_type=jnp.float32)
        scores = scores * HD ** (-0.5)
        mixed = [jnp.where(own, masked_score, scores[:, a:b])]
        if a > 0:
            mixed = [scores[:, :a]] + mixed
        if b < seq:
            mixed = mixed + [scores[:, b:]]
        scores = jnp.concatenate(mixed, axis=1)
        base = jnp.max(scores, axis=-1, keepdims=True).astype(jnp.bfloat16)
        weights = jnp.exp(scores - base.astype(jnp.float32))
        total = jnp.sum(weights, axis=-1, keepdims=True)
        result = jnp.dot(weights.astype(jnp.bfloat16), values, preferred_element_type=jnp.float32)
        result = (result / total).astype(jnp.bfloat16)
        total_high = total.astype(jnp.bfloat16)
        total_low = (total - total_high.astype(jnp.float32)).astype(jnp.bfloat16)
        so_send[i * per : (i + 1) * per] = jnp.concatenate(
            [result, base, total_high, total_low, self_pad], axis=1
        ).reshape(per, tok, LANES)
        start_some(so_send, so_recv, so_sems, i * per, per)

    for far in (0, HALF):
        for k in cuts:
            for i in range(1, HALF):
                g = piece_of((beside(i) + far) % LINE)
                gathered(g, k).wait_recv()
                to_other_core(c, g, k).start()

    end_exchange(cq_send, cq_recv, cq_sems)

    def twin_wait(q, _):
        for k in range(len(CUTS)):
            to_other_core(1 - c, q, k).wait_recv()
        return 0

    lax.fori_loop(0, LINE, twin_wait, 0)
    caption_rows = jnp.concatenate(
        [jnp.concatenate([caption[place(i, j)] for j in range(col_tiles)], axis=1) for i in range(row_tiles)], axis=0
    )
    head_states = lax.dot_general(
        caption_rows, kv_w_ref[...], contract_last, preferred_element_type=jnp.float32
    ).astype(jnp.bfloat16)
    prompt_keys, prompt_values = head_states[:, :HD], head_states[:, HD : 2 * HD]
    out_pad = jnp.zeros((chunk, LANES - HD), jnp.bfloat16)
    length = lengths_ref[source]
    visible = lax.broadcasted_iota(jnp.int32, (1, row_tiles * TILE), 1) < length
    cross_rows = cq_recv[...].reshape(seq, LANES)[:, :HD]
    for i in range(seq // chunk):
        a, b = i * chunk, (i + 1) * chunk
        scores = lax.dot_general(cross_rows[a:b], prompt_keys, contract_last, preferred_element_type=jnp.float32)
        scores = jnp.where(visible, scores * HD ** (-0.5), masked_score)
        weights = jnp.exp(scores - jnp.max(scores, axis=-1, keepdims=True))
        total = jnp.sum(weights, axis=-1, keepdims=True)
        result = jnp.dot(weights.astype(jnp.bfloat16), prompt_values, preferred_element_type=jnp.float32)
        result = (result / total).astype(jnp.bfloat16)
        co_send[i * per : (i + 1) * per] = jnp.concatenate([result, out_pad], axis=1).reshape(per, tok, LANES)
        start_some(co_send, co_recv, co_sems, i * per, per)

    end_exchange(so_send, so_recv, so_sems)
    merged = []
    for n in range(HEADS):
        block = so_recv[n].astype(jnp.float32)
        stale_base = block[:, HD : HD + 1]
        stale_total = block[:, HD + 1 : HD + 2] + block[:, HD + 2 : HD + 3]
        own_base = fresh_stats[n * tok : (n + 1) * tok, 0:1]
        own_total = fresh_stats[n * tok : (n + 1) * tok, 1:2]
        top = jnp.maximum(stale_base, own_base)
        stale_share = stale_total * jnp.exp(stale_base - top)
        own_scale = jnp.exp(own_base - top)
        both = stale_share + own_total * own_scale
        merged.append(
            block[:, :HD] * (stale_share / both) + fresh_blend[:, n * HD : (n + 1) * HD] * (own_scale / both)
        )
    out_ref[0] = jnp.concatenate(merged, axis=1)
    for pos in range(inner):

        @pl.when(pos < deep)
        def _():
            outward(pos).wait_send()

    def drain(pos, _):
        for k in range(len(SUM_CUTS)):

            @pl.when((pos > deep) & (deep < inner))
            def _():
                inward(pos, k).wait_send()

            @pl.when((pos > deep) & (deep == inner))
            def _():
                across(pos, k).wait_send()

        return 0

    lax.fori_loop(0, LINE, drain, 0)
    for pos in range(LINE):
        to_twin(pos).wait_send()
    for k in cuts:
        to_half(k).wait_send()
        for i in range(1, n_x):
            x_copy(i, h, k).wait_send()
            x_copy(i, 1 - h, k).wait_send()
        for i in range(1, n_y):
            y_copy(i, k).wait_send()
        for i in range(HALF):
            spread(here, i, i, k).wait_send()
        for i in range(1, HALF):
            spread(there, i, HALF - 1 + i, k).wait_send()

        def drain_twin(g, _):
            to_other_core(c, g, k).wait_send()
            return 0

        lax.fori_loop(0, LINE, drain_twin, 0)
    drain_exchange(cq_send, cq_recv, cq_sems)
    drain_exchange(sf_send, sf_recv, sf_sems)
    drain_exchange(so_send, so_recv, so_sems)
    end_exchange(co_send, co_recv, co_sems)
    out_ref[1] = jnp.concatenate([co_recv[n][:, :HD].astype(jnp.float32) for n in range(HEADS)], axis=1)

    drain_exchange(co_send, co_recv, co_sems)


def shards(
    dims,
    image_queries,
    cross_queries,
    fresh_kv,
    stale_kv,
    prompt_states,
    caption_weight,
    cross_kv_weight,
    prompt_lengths,
    prompt_route,
):
    n_y, n_h, n_x = dims
    operands = (
        prompt_states,
        caption_weight,
        cross_kv_weight.T,
        image_queries,
        cross_queries,
        fresh_kv,
        stale_kv,
    )
    tok, width = image_queries.shape[1:]
    piece = (TILES, TILE, LANES)
    dma = pltpu.SemaphoreType.DMA
    vmem = pl.BlockSpec(memory_space=pltpu.VMEM)
    smem = pl.BlockSpec(memory_space=pltpu.SMEM)
    f32, bf16 = jnp.float32, jnp.bfloat16
    sum_lines, lines, cuts = (LINE, len(SUM_CUTS)), (LINE, len(CUTS)), len(CUTS)
    hbm = pl.BlockSpec(memory_space=pltpu.HBM)
    by_head = pltpu.VMEM((HEADS, tok, LANES), bf16)
    by_head_wide = pltpu.VMEM((HEADS, tok, 2 * LANES), bf16)
    both = pl.pallas_call(
        functools.partial(kernel, dims),
        out_shape=pltpu.VMEM((2, tok, width), f32),
        in_specs=[smem, smem] + [hbm] * 7,
        out_specs=vmem,
        scratch_shapes=[
            *(pltpu.VMEM(array.shape, bf16) for array in operands),
            pltpu.VMEM((2, LINE, *piece), f32),
            pltpu.VMEM((LINE, *piece), f32),
            pltpu.VMEM((LINE, *piece), f32),
            pltpu.VMEM(piece, f32),
            pltpu.VMEM((HALF, *piece), f32),
            [pltpu.VMEM((n_x, n_h, m, TILE, LANES), bf16) for _, m in CUTS],
            [pltpu.VMEM((n_y, m, TILE, LANES), bf16) for _, m in CUTS],
            [pltpu.VMEM((n_y, m, TILE, LANES), bf16) for _, m in CUTS],
            pltpu.VMEM((2, LINE, *piece), bf16),
            by_head,
            by_head,
            by_head_wide,
            by_head_wide,
            by_head,
            by_head,
            by_head,
            by_head,
            pltpu.VMEM((HEADS * tok, LANES), f32),
            pltpu.VMEM((tok, width), f32),
            dma((len(operands),)),
            dma((2, LINE)),
            dma((2, *sum_lines)),
            dma((2, *sum_lines)),
            dma((2, HALF)),
            dma((2, cuts)),
            dma((2, cuts, n_h, n_x)),
            dma((2, cuts, n_y)),
            dma((LINE - 1, cuts)),
            dma(lines),
            dma((2, *lines)),
            dma((2, HEADS)),
            dma((2, HEADS)),
            dma((2, HEADS)),
            dma((2, HEADS)),
        ],
        compiler_params=pltpu.CompilerParams(
            collective_id=0, has_side_effects=True, vmem_limit_bytes=48 * 1024 * 1024
        ),
    )(prompt_route, prompt_lengths, *(pltpu.with_memory_space_constraint(a, pltpu.HBM) for a in operands))
    return both[0:1], both[1:2]


def solution(mesh, dims=(4, 2, 4)):
    in_specs = (
        P("req", "patch", None),
        P("req", "patch", None),
        P("req", "patch", None),
        P("req", "patch", None),
        P("req", None, "patch"),
        P("patch", None),
        P(None, "patch"),
        P(),
        P(),
    )
    out_specs = (P("req", "patch", None), P("req", "patch", None))
    return jax.shard_map(
        functools.partial(shards, dims), mesh=mesh, in_specs=in_specs, out_specs=out_specs, check_vma=False
    )
```

```python
import functools

import jax
import jax.numpy as jnp
from jax import lax
from jax.experimental import pallas as pl
from jax.experimental.pallas import tpu as pltpu
from jax.sharding import PartitionSpec as P

HEADS = 16
HD = 72
LANES = 128
TILE = 16
TILES = 11
LINE = 8
HALF = LINE // 2
masked_score = -1e30
MESH = pl.DeviceIdType.MESH
SUM_CUTS = ((0, 3), (3, 3), (6, 3), (9, 2))
CUTS = ((0, 6), (6, 5))


def far_first(size):
    return sorted(range(1, size), key=lambda i: -min(i, size - i))


def kernel(
    dims,
    route_ref,
    lengths_ref,
    prompt_hbm,
    caption_w_hbm,
    kv_w_hbm,
    image_q_hbm,
    cross_q_hbm,
    fresh_hbm,
    stale_hbm,
    out_ref,
    prompt_ref,
    caption_w_ref,
    kv_w_ref,
    image_q_ref,
    cross_q_ref,
    fresh_ref,
    stale_ref,
    part,
    sib_part,
    running,
    crossed,
    terms,
    routed,
    y_send,
    y_recv,
    caption,
    cq_send,
    cq_recv,
    sf_send,
    sf_recv,
    so_send,
    so_recv,
    co_send,
    co_recv,
    fresh_stats,
    fresh_blend,
    load_sems,
    sib_sems,
    run_sems,
    cross_sems,
    term_sems,
    h_sems,
    x_sems,
    y_sems,
    gather_send,
    gather_recv,
    twin_sems,
    cq_sems,
    sf_sems,
    so_sems,
    co_sems,
):
    n_y, n_h, n_x = dims
    me_r = lax.axis_index("req")
    me_p = lax.axis_index("patch")
    y = me_r // (n_h * n_x)
    h = (me_r // n_x) % n_h
    x = me_r % n_x
    z = me_p // 2
    c = me_p % 2
    u = z
    shift = h * HALF

    def piece_of(pos):
        return (pos + shift) % LINE

    def patch_peer(i):
        return {"patch": (me_p + i) % (2 * LINE)}

    twin = {"patch": 2 * z + 1 - c}
    half_peer = {"req": me_r + n_x * (1 - 2 * h), "patch": 2 * ((z + HALF) % LINE) + c}

    def x_peer(i):
        return {"req": me_r - x + (x + i) % n_x}

    def y_peer(i):
        return {"req": ((y + i) % n_y) * (n_h * n_x) + h * n_x + x}

    def copy(src, dst, send, recv, device):
        return pltpu.make_async_remote_copy(
            src_ref=src, dst_ref=dst, send_sem=send, recv_sem=recv, device_id=device, device_id_type=MESH
        )

    loads = [
        pltpu.make_async_copy(src, dst, load_sems.at[i])
        for i, (src, dst) in enumerate(
            (
                (prompt_hbm, prompt_ref),
                (caption_w_hbm, caption_w_ref),
                (cross_q_hbm, cross_q_ref),
                (image_q_hbm, image_q_ref),
                (stale_hbm, stale_ref),
                (fresh_hbm, fresh_ref),
                (kv_w_hbm, kv_w_ref),
            )
        )
    ]
    barrier = pltpu.get_barrier_semaphore()
    greeted = 0
    for device in (
        [patch_peer(i) for i in range(1, 2 * LINE)]
        + [half_peer]
        + [x_peer(i) for i in range(1, n_x)]
        + [y_peer(i) for i in range(1, n_y)]
    ):
        pl.semaphore_signal(barrier, inc=1, device_id=device, device_id_type=MESH)
        greeted += 1
    for load in loads:
        load.start()

    loads[0].wait()
    loads[1].wait()
    prompt = prompt_ref[0]
    rows = prompt.shape[0]
    row_tiles = -(-rows // TILE)
    prompt = jnp.concatenate(
        [prompt, jnp.zeros((row_tiles * TILE - rows, prompt.shape[1]), prompt.dtype)], axis=0
    )
    width = caption_w_ref.shape[1]
    col_tiles = width // LANES

    def place(i, j):
        piece, at = divmod(i * col_tiles + j, TILES)
        return piece // LINE, piece % LINE, at

    slots = [piece_of(g) for g in range(LINE)]

    group = 3
    for j0 in range(0, col_tiles, group):
        block = jnp.dot(
            prompt, caption_w_ref[:, j0 * LANES : (j0 + group) * LANES], preferred_element_type=jnp.float32
        )
        for i in range(row_tiles):
            for j in range(group):
                core, g, at = place(i, j0 + j)
                part[core, slots[g], at] = block[i * TILE : (i + 1) * TILE, j * LANES : (j + 1) * LANES]
    for t in range(row_tiles * col_tiles, 2 * LINE * TILES):
        part[t // (LINE * TILES), slots[(t // TILES) % LINE], t % TILES] = jnp.zeros((TILE, LANES), jnp.float32)

    left = u < HALF
    deep = jnp.where(left, u, LINE - 1 - u)

    def at(pos):
        return jnp.where(left, pos, LINE - 1 - pos)

    def to_twin(pos):
        return copy(part.at[1 - c, at(pos)], sib_part.at[at(pos)], sib_sems.at[0, pos], sib_sems.at[1, pos], twin)

    pl.semaphore_wait(barrier, greeted)
    for pos in reversed(range(LINE)):
        to_twin(pos).start()
    for load in loads[2:]:
        load.wait()

    tok = image_q_ref.shape[1]
    pad_c = jnp.zeros((tok, LANES - HD), jnp.bfloat16)
    pad_s = jnp.zeros((tok, 2 * LANES - 3 * HD), jnp.bfloat16)
    for n in range(HEADS):
        a, b = n * HD, (n + 1) * HD
        cq_send[n] = jnp.concatenate([cross_q_ref[0, :, a:b], pad_c], axis=1)
        sf_send[n] = jnp.concatenate(
            [
                image_q_ref[0, :, a:b],
                stale_ref[0, :, a:b],
                stale_ref[0, :, width + a : width + b],
                pad_s,
            ],
            axis=1,
        )

    def exchange(send, recv, sems, i):
        peer = (me_p + i) % (2 * LINE)
        return copy(send.at[peer], recv.at[me_p], sems.at[0, i], sems.at[1, i], {"patch": peer})

    def arrival(send, recv, sems, i):
        origin = (me_p - i + 2 * LINE) % (2 * LINE)
        return copy(send.at[origin], recv.at[origin], sems.at[0, i], sems.at[1, i], {"patch": origin})

    def start_exchange(send, recv, sems):
        recv[me_p] = send[me_p]

        def step(i, _):
            exchange(send, recv, sems, i).start()
            return 0

        lax.fori_loop(5, 12, step, 0)
        lax.fori_loop(1, 5, step, 0)
        lax.fori_loop(12, 2 * LINE, step, 0)

    def start_some(send, recv, sems, first, count):
        def step(n, _):
            @pl.when(n == me_p)
            def _():
                recv[n] = send[n]

            @pl.when(n != me_p)
            def _():
                exchange(send, recv, sems, (n - me_p + 2 * LINE) % (2 * LINE)).start()

            return 0

        lax.fori_loop(first, first + count, step, 0)

    def end_exchange(send, recv, sems):
        def step(i, _):
            arrival(send, recv, sems, i).wait_recv()
            return 0

        lax.fori_loop(1, 2 * LINE, step, 0)

    def drain_exchange(send, recv, sems):
        def step(i, _):
            exchange(send, recv, sems, i).wait_send()
            return 0

        lax.fori_loop(1, 2 * LINE, step, 0)

    start_exchange(cq_send, cq_recv, cq_sems)
    sums = part.at[c]

    def add_twin(pos):
        to_twin(pos).wait_recv()
        sums[at(pos)] = sums[at(pos)] + sib_part[at(pos)]

    inner = HALF - 1
    def at_device(pos):
        return {"patch": 2 * at(pos) + c}

    def sum_cut(k):
        a, m = SUM_CUTS[k]
        return pl.ds(a, m)

    def inward(pos, k):
        return copy(
            sums.at[at(pos), sum_cut(k)],
            running.at[at(pos), sum_cut(k)],
            run_sems.at[0, pos, k],
            run_sems.at[1, pos, k],
            at_device(jnp.minimum(deep + 1, inner)),
        )

    def across(pos, k):
        return copy(
            sums.at[at(pos), sum_cut(k)],
            crossed.at[sum_cut(k)],
            cross_sems.at[0, pos, k],
            cross_sems.at[1, 0, k],
            at_device(pos),
        )

    def outward(pos):
        return copy(
            sums.at[at(pos)], terms.at[deep], term_sems.at[0, pos], term_sems.at[1, deep], at_device(pos)
        )

    def term_arrival(pos):
        return copy(sums.at[u], terms.at[pos], term_sems.at[0, 0], term_sems.at[1, pos], at_device(pos))

    def first_step(t, _):
        pos = LINE - 1 - t
        add_twin(pos)

        @pl.when(pos < deep)
        def _():
            outward(pos).start()

        return 0

    @pl.when(deep > 0)
    def _():
        lax.fori_loop(0, LINE, first_step, 0)

    def reduce_step(t, _):
        pos = LINE - 1 - t

        @pl.when(deep == 0)
        def _():
            add_twin(pos)

        @pl.when(pos >= deep)
        def _():
            for k in range(len(SUM_CUTS)):

                @pl.when(deep > 0)
                def _():
                    inward(pos, k).wait_recv()
                    sums[at(pos), sum_cut(k)] = sums[at(pos), sum_cut(k)] + running[at(pos), sum_cut(k)]

                @pl.when((pos > deep) & (deep < inner))
                def _():
                    inward(pos, k).start()

                @pl.when((pos > deep) & (deep == inner))
                def _():
                    across(pos, k).start()

        return 0

    lax.fori_loop(0, LINE, reduce_step, 0)
    for pos in range(1, HALF):

        @pl.when(pos > deep)
        def _():
            term_arrival(pos).wait_recv()
            sums[u] = sums[u] + terms[pos]

    for k in range(len(SUM_CUTS)):
        across(inner + 1, k).wait_recv()

    def to_half(k):
        ref = routed[k].at[x, h]
        return copy(ref, ref, h_sems.at[0, k], h_sems.at[1, k], half_peer)

    def half_arrival(k):
        ref = routed[k].at[x, 1 - h]
        return copy(ref, ref, h_sems.at[0, k], h_sems.at[1, k], half_peer)

    def x_copy(i, half, k):
        ref = routed[k].at[x, half]
        return copy(ref, ref, x_sems.at[0, k, half, i], x_sems.at[1, k, half, i], x_peer(i))

    def x_arrival(i, half, k):
        ref = routed[k].at[(x - i + n_x) % n_x, half]
        return copy(ref, ref, x_sems.at[0, k, half, i], x_sems.at[1, k, half, i], x_peer(i))

    def wanted(i, k):
        source = route_ref[((y + i) % n_y) * (n_h * n_x) + h * n_x + x]
        return routed[k][lax.rem(source, n_x), lax.rem(lax.div(source, n_x), n_h)]

    def y_copy(i, k):
        return copy(y_send[k].at[i], y_recv[k].at[y], y_sems.at[0, k, i], y_sems.at[1, k, i], y_peer(i))

    def y_arrival(i, k):
        ref = y_recv[k].at[(y - i + n_y) % n_y]
        return copy(ref, ref, y_sems.at[0, k, i], y_sems.at[1, k, i], y_peer(i))

    here = piece_of(u)
    there = piece_of((u + HALF) % LINE)

    def beside(i):
        return (u // HALF) * HALF + (u + i) % HALF

    def tiles_of(core, g, k):
        a, m = CUTS[k]
        return caption.at[core, g, pl.ds(a, m)]

    def spread(g, i, n, k):
        pos = beside(i) if i else (u + HALF) % LINE
        ref = tiles_of(c, g, k)
        return copy(ref, ref, gather_send.at[n, k], gather_recv.at[g, k], {"patch": 2 * pos + c})

    def gathered(g, k):
        ref = tiles_of(c, g, k)
        return copy(ref, ref, gather_send.at[0, k], gather_recv.at[g, k], twin)

    def to_other_core(core, g, k):
        ref = tiles_of(core, g, k)
        return copy(ref, ref, twin_sems.at[0, g, k], twin_sems.at[1, g, k], twin)

    cuts = range(len(CUTS))
    for k, (a, m) in enumerate(CUTS):
        piece = sums[u, a : a + m] + crossed[a : a + m]
        piece = jax.nn.gelu(piece, approximate=True).astype(jnp.bfloat16)
        routed[k][x, h] = piece
        to_half(k).start()
        for i in far_first(n_x):
            x_copy(i, h, k).start()
    seq = 2 * LINE * tok
    contract_last = (((1,), (1,)), ((), ()))
    chunk = LANES
    per = chunk // tok
    zero = jnp.zeros((), jnp.bfloat16)
    head_of = lax.broadcasted_iota(jnp.int32, (tok, width), 1) // HD

    def apart(rows):
        return jnp.concatenate([jnp.where(head_of == n, rows, zero) for n in range(HEADS)], axis=0)

    fresh_scores = lax.dot_general(
        apart(image_q_ref[0]), fresh_ref[0, :, :width], contract_last, preferred_element_type=jnp.float32
    )
    fresh_scores = fresh_scores * HD ** (-0.5)
    fresh_base = jnp.max(fresh_scores, axis=-1, keepdims=True)
    fresh_weights = jnp.exp(fresh_scores - fresh_base)
    fresh_total = jnp.sum(fresh_weights, axis=-1, keepdims=True)
    fresh_weights = fresh_weights.astype(jnp.bfloat16)
    fresh_stats[:, 0:1] = fresh_base
    fresh_stats[:, 1:2] = fresh_total
    fresh_blend[...] = jnp.dot(
        jnp.concatenate([fresh_weights[n * tok : (n + 1) * tok] for n in range(HEADS)], axis=1),
        apart(fresh_ref[0, :, width:]),
        preferred_element_type=jnp.float32,
    )

    for k in cuts:
        half_arrival(k).wait_recv()
        for i in far_first(n_x):
            x_copy(i, 1 - h, k).start()
    start_exchange(sf_send, sf_recv, sf_sems)
    for k in cuts:
        for i in range(1, n_x):
            x_arrival(i, h, k).wait_recv()
            x_arrival(i, 1 - h, k).wait_recv()
        for i in far_first(n_y):
            y_send[k][i] = wanted(i, k)
            y_copy(i, k).start()
        y_recv[k][y] = wanted(0, k)
    source = route_ref[me_r]
    for k, (a, m) in enumerate(CUTS):
        for i in range(1, n_y):
            y_arrival(i, k).wait_recv()
        caption[c, here, a : a + m] = y_recv[k][lax.div(source, n_h * n_x)]
        spread(here, 0, 0, k).start()
    for k in cuts:
        for i in range(1, HALF):
            spread(here, i, i, k).start()
        to_other_core(c, here, k).start()

    for k in cuts:
        gathered(there, k).wait_recv()
        for i in range(1, HALF):
            spread(there, i, HALF - 1 + i, k).start()
        to_other_core(c, there, k).start()
    end_exchange(sf_send, sf_recv, sf_sems)
    whole = sf_recv[...].reshape(seq, 2 * LANES)
    queries, keys, values = whole[:, :HD], whole[:, HD : 2 * HD], whole[:, 2 * HD : 3 * HD]
    own = (
        lax.broadcasted_iota(jnp.int32, (chunk, chunk), 0) // tok
        == lax.broadcasted_iota(jnp.int32, (chunk, chunk), 1) // tok
    )
    self_pad = jnp.zeros((chunk, LANES - HD - 3), jnp.bfloat16)
    for i in range(seq // chunk):
        a, b = i * chunk, (i + 1) * chunk
        scores = lax.dot_general(queries[a:b], keys, contract_last, preferred_element_type=jnp.float32)
        scores = scores * HD ** (-0.5)
        mixed = [jnp.where(own, masked_score, scores[:, a:b])]
        if a > 0:
            mixed = [scores[:, :a]] + mixed
        if b < seq:
            mixed = mixed + [scores[:, b:]]
        scores = jnp.concatenate(mixed, axis=1)
        base = jnp.max(scores, axis=-1, keepdims=True).astype(jnp.bfloat16)
        weights = jnp.exp(scores - base.astype(jnp.float32))
        total = jnp.sum(weights, axis=-1, keepdims=True)
        result = jnp.dot(weights.astype(jnp.bfloat16), values, preferred_element_type=jnp.float32)
        result = (result / total).astype(jnp.bfloat16)
        total_high = total.astype(jnp.bfloat16)
        total_low = (total - total_high.astype(jnp.float32)).astype(jnp.bfloat16)
        so_send[i * per : (i + 1) * per] = jnp.concatenate(
            [result, base, total_high, total_low, self_pad], axis=1
        ).reshape(per, tok, LANES)
        start_some(so_send, so_recv, so_sems, i * per, per)

    for far in (0, HALF):
        for k in cuts:
            for i in range(1, HALF):
                g = piece_of((beside(i) + far) % LINE)
                gathered(g, k).wait_recv()
                to_other_core(c, g, k).start()

    end_exchange(cq_send, cq_recv, cq_sems)

    def twin_wait(q, _):
        for k in range(len(CUTS)):
            to_other_core(1 - c, q, k).wait_recv()
        return 0

    lax.fori_loop(0, LINE, twin_wait, 0)
    caption_rows = jnp.concatenate(
        [jnp.concatenate([caption[place(i, j)] for j in range(col_tiles)], axis=1) for i in range(row_tiles)], axis=0
    )
    head_states = lax.dot_general(
        caption_rows, kv_w_ref[...], contract_last, preferred_element_type=jnp.float32
    ).astype(jnp.bfloat16)
    prompt_keys, prompt_values = head_states[:, :HD], head_states[:, HD : 2 * HD]
    out_pad = jnp.zeros((chunk, LANES - HD), jnp.bfloat16)
    length = lengths_ref[source]
    visible = lax.broadcasted_iota(jnp.int32, (1, row_tiles * TILE), 1) < length
    cross_rows = cq_recv[...].reshape(seq, LANES)[:, :HD]
    for i in range(seq // chunk):
        a, b = i * chunk, (i + 1) * chunk
        scores = lax.dot_general(cross_rows[a:b], prompt_keys, contract_last, preferred_element_type=jnp.float32)
        scores = jnp.where(visible, scores * HD ** (-0.5), masked_score)
        weights = jnp.exp(scores - jnp.max(scores, axis=-1, keepdims=True))
        total = jnp.sum(weights, axis=-1, keepdims=True)
        result = jnp.dot(weights.astype(jnp.bfloat16), prompt_values, preferred_element_type=jnp.float32)
        result = (result / total).astype(jnp.bfloat16)
        co_send[i * per : (i + 1) * per] = jnp.concatenate([result, out_pad], axis=1).reshape(per, tok, LANES)
        start_some(co_send, co_recv, co_sems, i * per, per)

    end_exchange(so_send, so_recv, so_sems)
    merged = []
    for n in range(HEADS):
        block = so_recv[n].astype(jnp.float32)
        stale_base = block[:, HD : HD + 1]
        stale_total = block[:, HD + 1 : HD + 2] + block[:, HD + 2 : HD + 3]
        own_base = fresh_stats[n * tok : (n + 1) * tok, 0:1]
        own_total = fresh_stats[n * tok : (n + 1) * tok, 1:2]
        top = jnp.maximum(stale_base, own_base)
        stale_share = stale_total * jnp.exp(stale_base - top)
        own_scale = jnp.exp(own_base - top)
        both = stale_share + own_total * own_scale
        merged.append(
            block[:, :HD] * (stale_share / both) + fresh_blend[:, n * HD : (n + 1) * HD] * (own_scale / both)
        )
    out_ref[0] = jnp.concatenate(merged, axis=1)
    for pos in range(inner):

        @pl.when(pos < deep)
        def _():
            outward(pos).wait_send()

    def drain(pos, _):
        for k in range(len(SUM_CUTS)):

            @pl.when((pos > deep) & (deep < inner))
            def _():
                inward(pos, k).wait_send()

            @pl.when((pos > deep) & (deep == inner))
            def _():
                across(pos, k).wait_send()

        return 0

    lax.fori_loop(0, LINE, drain, 0)
    for pos in range(LINE):
        to_twin(pos).wait_send()
    for k in cuts:
        to_half(k).wait_send()
        for i in range(1, n_x):
            x_copy(i, h, k).wait_send()
            x_copy(i, 1 - h, k).wait_send()
        for i in range(1, n_y):
            y_copy(i, k).wait_send()
        for i in range(HALF):
            spread(here, i, i, k).wait_send()
        for i in range(1, HALF):
            spread(there, i, HALF - 1 + i, k).wait_send()

        def drain_twin(g, _):
            to_other_core(c, g, k).wait_send()
            return 0

        lax.fori_loop(0, LINE, drain_twin, 0)
    drain_exchange(cq_send, cq_recv, cq_sems)
    drain_exchange(sf_send, sf_recv, sf_sems)
    drain_exchange(so_send, so_recv, so_sems)
    end_exchange(co_send, co_recv, co_sems)
    out_ref[1] = jnp.concatenate([co_recv[n][:, :HD].astype(jnp.float32) for n in range(HEADS)], axis=1)

    drain_exchange(co_send, co_recv, co_sems)


def shards(
    dims,
    image_queries,
    cross_queries,
    fresh_kv,
    stale_kv,
    prompt_states,
    caption_weight,
    cross_kv_weight,
    prompt_lengths,
    prompt_route,
):
    n_y, n_h, n_x = dims
    operands = (
        prompt_states,
        caption_weight,
        cross_kv_weight.T,
        image_queries,
        cross_queries,
        fresh_kv,
        stale_kv,
    )
    tok, width = image_queries.shape[1:]
    piece = (TILES, TILE, LANES)
    dma = pltpu.SemaphoreType.DMA
    vmem = pl.BlockSpec(memory_space=pltpu.VMEM)
    smem = pl.BlockSpec(memory_space=pltpu.SMEM)
    f32, bf16 = jnp.float32, jnp.bfloat16
    sum_lines, lines, cuts = (LINE, len(SUM_CUTS)), (LINE, len(CUTS)), len(CUTS)
    hbm = pl.BlockSpec(memory_space=pltpu.HBM)
    by_head = pltpu.VMEM((HEADS, tok, LANES), bf16)
    by_head_wide = pltpu.VMEM((HEADS, tok, 2 * LANES), bf16)
    both = pl.pallas_call(
        functools.partial(kernel, dims),
        out_shape=pltpu.VMEM((2, tok, width), f32),
        in_specs=[smem, smem] + [hbm] * 7,
        out_specs=vmem,
        scratch_shapes=[
            *(pltpu.VMEM(array.shape, bf16) for array in operands),
            pltpu.VMEM((2, LINE, *piece), f32),
            pltpu.VMEM((LINE, *piece), f32),
            pltpu.VMEM((LINE, *piece), f32),
            pltpu.VMEM(piece, f32),
            pltpu.VMEM((HALF, *piece), f32),
            [pltpu.VMEM((n_x, n_h, m, TILE, LANES), bf16) for _, m in CUTS],
            [pltpu.VMEM((n_y, m, TILE, LANES), bf16) for _, m in CUTS],
            [pltpu.VMEM((n_y, m, TILE, LANES), bf16) for _, m in CUTS],
            pltpu.VMEM((2, LINE, *piece), bf16),
            by_head,
            by_head,
            by_head_wide,
            by_head_wide,
            by_head,
            by_head,
            by_head,
            by_head,
            pltpu.VMEM((HEADS * tok, LANES), f32),
            pltpu.VMEM((tok, width), f32),
            dma((len(operands),)),
            dma((2, LINE)),
            dma((2, *sum_lines)),
            dma((2, *sum_lines)),
            dma((2, HALF)),
            dma((2, cuts)),
            dma((2, cuts, n_h, n_x)),
            dma((2, cuts, n_y)),
            dma((LINE - 1, cuts)),
            dma(lines),
            dma((2, *lines)),
            dma((2, HEADS)),
            dma((2, HEADS)),
            dma((2, HEADS)),
            dma((2, HEADS)),
        ],
        compiler_params=pltpu.CompilerParams(
            collective_id=0, has_side_effects=True, vmem_limit_bytes=48 * 1024 * 1024
        ),
    )(prompt_route, prompt_lengths, *(pltpu.with_memory_space_constraint(a, pltpu.HBM) for a in operands))
    return both[0:1], both[1:2]


def solution(mesh, dims=(4, 2, 4)):
    in_specs = (
        P("req", "patch", None),
        P("req", "patch", None),
        P("req", "patch", None),
        P("req", "patch", None),
        P("req", None, "patch"),
        P("patch", None),
        P(None, "patch"),
        P(),
        P(),
    )
    out_specs = (P("req", "patch", None), P("req", "patch", None))
    return jax.shard_map(
        functools.partial(shards, dims), mesh=mesh, in_specs=in_specs, out_specs=out_specs, check_vma=False
    )
```
